32 devices in a mesh: ctx: 8 (over z, core), fsdp: 4 (over y, x).
Axes of the slice: x: 2, y: 2, z: 4, core: 2. Of those that a mesh axis runs over, the one named last changes fastest.
Arguments:
- tokens: bfloat16 [16, 1536, 768], P('fsdp', 'ctx'), may hold values from -6 to 6
- lengths: int32 [16], P('fsdp'), may hold values from 384 to 1536, as said below
- cotangent: bfloat16 [16, 1536, 768], P('fsdp', 'ctx'), may hold values from -6 to 6
- qkv_weight: bfloat16 [768, 2304], P('fsdp'), may hold values from -0.21875 to 0.21875
- qkv_bias: bfloat16 [2304], P('fsdp'), may hold values from -3 to 3
- out_weight: bfloat16 [768, 768], P('fsdp'), may hold values from -0.875 to 0.875
- out_bias: bfloat16 [768], P('fsdp'), may hold values from -2 to 2
- up_weight: bfloat16 [768, 3072], P('fsdp'), may hold values from -0.21875 to 0.21875
- up_bias: bfloat16 [3072], P('fsdp'), may hold values from -3 to 3
- down_weight: bfloat16 [3072, 768], P('fsdp'), may hold values from -0.109375 to 0.109375
- down_bias: bfloat16 [768], P('fsdp'), may hold values from -2 to 2
- attn_gain: bfloat16 [768], P('fsdp'), may hold values from 0.099609375 to 1.8984375
- attn_shift: bfloat16 [768], P('fsdp'), may hold values from -2 to 2
- mlp_gain: bfloat16 [768], P('fsdp'), may hold values from 0.099609375 to 1.8984375
- mlp_shift: bfloat16 [768], P('fsdp'), may hold values from -2 to 2
Outputs:
- layer_out: bfloat16 [16, 1536, 768], P('fsdp', 'ctx')
- tokens_grad: float32 [16, 1536, 768], P('fsdp', 'ctx')
- qkv_weight_grad: float32 [768, 2304], P('fsdp')
- qkv_bias_grad: float32 [2304], P('fsdp')
- out_weight_grad: float32 [768, 768], P('fsdp')
- out_bias_grad: float32 [768], P('fsdp')
- up_weight_grad: float32 [768, 3072], P('fsdp')
- up_bias_grad: float32 [3072], P('fsdp')
- down_weight_grad: float32 [3072, 768], P('fsdp')
- down_bias_grad: float32 [768], P('fsdp')
- attn_gain_grad: float32 [768], P('fsdp')
- attn_shift_grad: float32 [768], P('fsdp')
- mlp_gain_grad: float32 [768], P('fsdp')
- mlp_shift_grad: float32 [768], P('fsdp')
The draws below stay inside these ranges and needn't reach their ends.
Inputs may be any that keep to these rules, and one draw needn't show every extreme that they name: `lengths`: in each group of 4 sequences on one index of fsdp, one sequence chosen by the seed has length 1536.
All inputs are finite; a program needn't handle non-finite values.
Results may differ from the reference program's by a relative error of at most 0.02.
Values may be sent and summed in bfloat16 or wider, within the bound.
No kernel may reach another device: no remote copies, remote signals or barrier semaphores. Data moves between devices by JAX's collectives and lax.ppermute only.
A program may use at most 256 MiB of HBM per device.

```python
import math
import jax
import jax.numpy as jnp
from jax import lax

D = 768
HEADS = 12
HEAD_DIM = 64
FF = 3072
ROTARY = 16
SEQS = 4
LEN = 1536
SEQS_ALL = 16
N_FSDP = 4


def draw_lengths(key, part):
    key = jax.random.fold_in(key, 11)
    pick_key, length_key = jax.random.split(key)
    values_drawn = jax.random.randint(length_key, (N_FSDP, SEQS), LEN // 4, LEN + 1)
    chosen = jax.random.randint(pick_key, (N_FSDP, 1), 0, SEQS)
    full_mask = jnp.arange(SEQS)[None, :] == chosen
    return jnp.where(full_mask, LEN, values_drawn).reshape(SEQS_ALL).astype(jnp.int32)


def shard_levels(stream_key, extent, shards, least, top_value):
    loudness = 1.0
    for position, blocks in shards:
        heights = jax.random.uniform(jax.random.fold_in(jax.random.fold_in(stream_key, 6), position), (blocks,), jnp.float32, least / len(shards), top_value / len(shards))
        loudness = loudness * jnp.repeat(jnp.exp(heights), extent[position] // blocks).reshape((-1,) + (1,) * (len(extent) - 1 - position))
    return loudness


def normal_values(own_key, dims, scale, most, pieces=(), kind=jnp.bfloat16):
    entries = scale * jax.random.normal(own_key, dims, jnp.float32)
    if pieces:
        entries = entries * shard_levels(own_key, dims, pieces, -0.22, 0.18)
    return jnp.clip(entries, -most, most).astype(kind)


def setup_inputs(seed: int = 0) -> dict:
    key_of = jax.random.split(jax.random.key(seed), 16)
    return {
        "tokens": normal_values(key_of[0], (SEQS_ALL, LEN, D), 1.0, 6.0, ((0, 4), (1, 8))),
        "lengths": draw_lengths(jax.random.fold_in(key_of[15], 71), 0),
        "cotangent": normal_values(key_of[2], (SEQS_ALL, LEN, D), 1.0, 6.0, ((0, 4), (1, 8))),
        "qkv_weight": normal_values(key_of[3], (D, 3 * D), D ** -0.5, 0.21875, ((0, 4),)),
        "qkv_bias": normal_values(key_of[4], (3 * D,), 0.5, 3.0, ((0, 4),)),
        "out_weight": normal_values(key_of[5], (D, D), (D // 16) ** -0.5, 0.875, ((0, 4),)),
        "out_bias": normal_values(key_of[6], (D,), 0.3, 2.0, ((0, 4),)),
        "up_weight": normal_values(key_of[7], (D, FF), D ** -0.5, 0.21875, ((0, 4),)),
        "up_bias": normal_values(key_of[8], (FF,), 0.5, 3.0, ((0, 4),)),
        "down_weight": normal_values(key_of[9], (FF, D), FF ** -0.5, 0.109375, ((0, 4),)),
        "down_bias": normal_values(key_of[10], (D,), 0.3, 2.0, ((0, 4),)),
        "attn_gain": jnp.clip(1.0 + 0.18 * jax.random.normal(key_of[11], (D,), jnp.float32), 0.099609375, 1.8984375).astype(jnp.bfloat16),
        "attn_shift": normal_values(key_of[12], (D,), 0.3, 2.0, ((0, 4),)),
        "mlp_gain": jnp.clip(1.0 + 0.18 * jax.random.normal(key_of[13], (D,), jnp.float32), 0.099609375, 1.8984375).astype(jnp.bfloat16),
        "mlp_shift": normal_values(key_of[14], (D,), 0.3, 2.0, ((0, 4),)),
    }


@jax.custom_vjp
def low(v):
    return lax.optimization_barrier(v.astype(jnp.bfloat16)).astype(jnp.float32)

@jax.custom_vjp
def low_back(v):
    return v

def low_keep(v):
    return (low(v), None)

def low_pass(kept, grad):
    return (grad,)

def back_keep(v):
    return (v, None)

def back_low(kept, grad):
    return (low(grad),)
low.defvjp(low_keep, low_pass)
low_back.defvjp(back_keep, back_low)
norm_eps = 1e-05
masked_score = -1e+30
rope_base = 10000.0
highest = lax.Precision.HIGHEST

def tables(positions):
    half_rot = ROTARY // 2
    frequency = rope_base ** (-2.0 * jnp.arange(half_rot, dtype=jnp.float32) / ROTARY)
    angles = positions.astype(jnp.float32)[:, None] * frequency[None, :]
    return (jnp.cos(angles)[:, None, :], jnp.sin(angles)[:, None, :])

def rotate(field, cosine, sine):
    half_rot = ROTARY // 2
    first_half = field[..., :half_rot]
    second_half = field[..., half_rot:ROTARY]
    return jnp.concatenate([first_half * cosine - second_half * sine, second_half * cosine + first_half * sine, field[..., ROTARY:]], -1)

def attend(queries, keys_all, values_all, seq_length):
    block_rows = math.gcd(LEN, 512)
    key_pos = jnp.arange(LEN).astype(jnp.int32)
    att_scale = HEAD_DIM ** (-0.5)

    def one_block(block_index):
        start_row = (block_index * block_rows).astype(jnp.int32)
        query_block = lax.dynamic_slice_in_dim(queries, start_row, block_rows, 0)
        scores = jnp.einsum('qhd,khd->hqk', query_block, keys_all, precision=highest) * att_scale
        scores = low_back(scores)
        query_pos = start_row + jnp.arange(block_rows).astype(jnp.int32)
        allowed = (key_pos[None, :] <= query_pos[:, None]) & (key_pos[None, :] < seq_length)
        scores = jnp.where(allowed[None], scores, masked_score)
        probs = low(jax.nn.softmax(scores, -1))
        return jnp.einsum('hqk,khd->qhd', probs, values_all, precision=highest)
    blocks_out = lax.map(jax.checkpoint(one_block), jnp.arange(LEN // block_rows).astype(jnp.int32))
    return blocks_out.reshape(LEN, HEADS, HEAD_DIM)

def layer(tok_rows, seq_length, qkv_w, qkv_b, out_w, out_b, up_w, up_b, down_w, down_b, attn_g, attn_s, mlp_g, mlp_s):
    center = tok_rows - lax.optimization_barrier(jnp.mean(tok_rows, -1, keepdims=True))
    spread = lax.optimization_barrier(jnp.mean(center * center, -1, keepdims=True))
    normed = center * lax.rsqrt(spread + norm_eps)
    attn_in = low(normed * attn_g + attn_s)
    mlp_in = low(normed * mlp_g + mlp_s)
    projected = low_back(jnp.dot(attn_in, qkv_w, precision=highest) + qkv_b)
    cosine, sine = tables(jnp.arange(LEN).astype(jnp.int32))
    head_shape = (LEN, HEADS, HEAD_DIM)
    queries = low(rotate(projected[:, :D].reshape(head_shape), cosine, sine))
    keys_all = low(rotate(projected[:, D:2 * D].reshape(head_shape), cosine, sine))
    values_all = low(projected[:, 2 * D:].reshape(head_shape))
    mixed = low(low_back(attend(queries, keys_all, values_all, seq_length))).reshape(LEN, D)
    attn_out = jnp.dot(mixed, out_w, precision=highest) + out_b
    pre_act = low_back(jnp.dot(mlp_in, up_w, precision=highest) + up_b)
    hidden = low(jax.nn.gelu(pre_act, approximate=False))
    mlp_out = jnp.dot(hidden, down_w, precision=highest) + down_b
    return tok_rows + attn_out + mlp_out

def reference(tokens, lengths, cotangent, qkv_weight, qkv_bias, out_weight, out_bias, up_weight, up_bias, down_weight, down_bias, attn_gain, attn_shift, mlp_gain, mlp_shift):
    weights = tuple((member.astype(jnp.float32) for member in (qkv_weight, qkv_bias, out_weight, out_bias, up_weight, up_bias, down_weight, down_bias, attn_gain, attn_shift, mlp_gain, mlp_shift)))

    def per_sequence(totals, inputs):
        seq_rows, seq_length, seq_cot = inputs

        def forward(rows_in, params_tuple):
            return layer(rows_in, seq_length, *params_tuple)
        outputs, pullback = jax.vjp(forward, seq_rows.astype(jnp.float32), weights)
        rows_grad, param_grads = pullback(seq_cot.astype(jnp.float32))
        totals = tuple((running + grad_part for running, grad_part in zip(totals, param_grads)))
        return (totals, (outputs.astype(jnp.bfloat16), rows_grad))
    zeros_init = tuple((jnp.zeros(member.shape, jnp.float32) for member in weights))
    sums, (layer_out, tokens_grad) = lax.scan(per_sequence, zeros_init, (tokens, lengths, cotangent))
    return (layer_out, tokens_grad, sums[0], sums[1], sums[2], sums[3], sums[4], sums[5], sums[6], sums[7], sums[8], sums[9], sums[10], sums[11])
```

```python
import functools

import jax
import jax.numpy as jnp
from jax import lax
from jax.experimental import pallas as pl
from jax.experimental.pallas import tpu as pltpu
from jax.sharding import PartitionSpec as P

D = 768
HEADS = 12
HEAD_DIM = 64
FF = 3072
ROTARY = 16

norm_eps = 1e-05
rope_base = 10000.0
inv_sqrt_two = 0.7071067811865476
inv_sqrt_tau = 0.3989422804014327
log2_e = 1.4426950408889634
masked_bias = -1e30
score_scale = HEAD_DIM ** (-0.5)

f32 = jnp.float32
bf16 = jnp.bfloat16
NT = (((1,), (1,)), ((), ()))
NN = (((1,), (0,)), ((), ()))
TN = (((0,), (0,)), ((), ()))


def dot(a, b, dims=NN):
    return lax.dot_general(a, b, dims, preferred_element_type=f32)


def attention_kernel(
    length_ref,
    attn_in_ref,
    cot_ref,
    w_ref,
    bias_ref,
    out_w_ref,
    cos_ref,
    sin_lo_ref,
    sin_hi_ref,
    mixed_ref,
    dproj_ref,
    q_s,
    k_a,
    k_b,
    v_a,
    v_b,
    kt_a,
    kt_b,
    vt_a,
    vt_b,
    do_s,
    dk_s,
    dv_s,
    *,
    seq_len,
    rows,
    groups,
):
    live = length_ref[0]
    lane = lax.broadcasted_iota(jnp.int32, (rows, 128), 1)
    low = lane < HEAD_DIM

    def rope(x, span, back):
        up = pltpu.roll(x, 120, 1) * sin_lo_ref[span, :]
        down = pltpu.roll(x, 8, 1) * sin_hi_ref[span, :]
        turned = x * cos_ref[span, :]
        return turned - up - down if back else turned + up + down

    def project(j, carry):
        start = pl.multiple_of(j * rows, rows)
        span = pl.ds(start, rows)
        proj = dot(attn_in_ref[span, :], w_ref[...]) + bias_ref[...]
        q_s[span, :] = (rope(proj[:, :128], span, False) * (score_scale * log2_e)).astype(bf16)
        keys = rope(proj[:, 128:256], span, False)
        values = proj[:, 256:]
        key_pos = start + lax.broadcasted_iota(jnp.int32, (rows, 128), 0)
        dead = jnp.where(key_pos < live, 0.0, masked_bias)
        ka = jnp.where(low, keys, jnp.where(lane == HEAD_DIM, dead, 0.0))
        kb = jnp.where(low, jnp.where(lane == 0, dead, 0.0), keys)
        va = jnp.where(low, values, 1.0)
        vb = jnp.where(low, 1.0, values)
        for src, plain, turned in (
            (ka, k_a, kt_a),
            (kb, k_b, kt_b),
            (va, v_a, vt_a),
            (vb, v_b, vt_b),
        ):
            plain[span, :] = src.astype(bf16)
            turned[:, span] = src.T.astype(bf16)
        do_s[span, :] = dot(cot_ref[span, :], out_w_ref[...], NT)
        return carry

    lax.fori_loop(0, seq_len // rows, project, 0)

    def attend(q0, nk, group_keys, first):
        q_span = pl.ds(q0, rows)
        queries = q_s[q_span, :].astype(f32)
        zero = jnp.zeros_like(queries)
        qa = jnp.where(low, queries, zero).astype(bf16)
        qb = jnp.where(low, zero, queries).astype(bf16)
        qa1 = jnp.where(low, queries, jnp.where(lane == HEAD_DIM, 1.0, 0.0)).astype(bf16)
        qb1 = jnp.where(low, jnp.where(lane == 0, 1.0, 0.0), queries).astype(bf16)
        edge = nk - group_keys
        key_pos = edge + lax.broadcasted_iota(jnp.int32, (group_keys, rows), 0)
        query_pos = q0 + lax.broadcasted_iota(jnp.int32, (group_keys, rows), 1)
        causal = key_pos <= query_pos
        probs = []
        mixes = []
        for keys, turned, q1 in ((k_a, vt_a, qa1), (k_b, vt_b, qb1)):
            s_edge = dot(keys[edge:nk, :], q1, NT)
            s_edge = jnp.where(causal, s_edge, masked_bias)
            best = jnp.max(s_edge, 0, keepdims=True)
            if edge:
                s_body = dot(keys[:edge, :], q1, NT)
                best = jnp.maximum(best, jnp.max(s_body, 0, keepdims=True))
                p = jnp.concatenate(
                    [
                        jnp.exp2(s_body - best).astype(bf16),
                        jnp.exp2(s_edge - best).astype(bf16),
                    ],
                    0,
                )
            else:
                p = jnp.exp2(s_edge - best).astype(bf16)
            probs.append(p)
            mixes.append(dot(turned[:, :nk], p).T)
        unscaled = jnp.where(low, mixes[0], mixes[1])
        denom = pltpu.roll(jnp.where(low, mixes[1], mixes[0]), HEAD_DIM, 1)
        inv = 1.0 / denom
        out = unscaled * inv
        mixed_ref[q_span, :] = out.astype(bf16)
        grad = (do_s[q_span, :] * inv).astype(bf16)
        grad_f = grad.astype(f32)
        prod = grad_f * out
        da = jnp.sum(jnp.where(low, prod, 0.0), 1, keepdims=True)
        db = jnp.sum(jnp.where(low, 0.0, prod), 1, keepdims=True)
        da_hi = da.astype(bf16).astype(f32)
        db_hi = db.astype(bf16).astype(f32)
        ga = jnp.where(low, grad_f, 0.0)
        gb = jnp.where(low, 0.0, grad_f)
        ga1 = jnp.where(
            lane == HEAD_DIM, -da_hi, jnp.where(lane == HEAD_DIM + 1, da_hi - da, ga)
        ).astype(bf16)
        gb1 = jnp.where(lane == 0, -db_hi, jnp.where(lane == 1, db_hi - db, gb)).astype(bf16)
        ga = ga.astype(bf16)
        gb = gb.astype(bf16)
        grad_scores = []
        for p, values, g1 in zip(probs, (v_a, v_b), (ga1, gb1)):
            dp = dot(values[:nk, :], g1, NT)
            grad_scores.append((p.astype(f32) * dp).astype(bf16))
        dq = dot(kt_a[:, :nk], grad_scores[0]) + dot(kt_b[:, :nk], grad_scores[1])
        dproj_ref[q_span, :128] = rope(dq.T * score_scale, q_span, True).astype(bf16)
        dk = dot(jnp.concatenate(grad_scores, 1), jnp.concatenate([qa, qb], 0))
        dv = dot(jnp.concatenate(probs, 1), jnp.concatenate([ga, gb], 0))
        if first:
            dk_s[:nk, :] = dk
            dv_s[:nk, :] = dv
        else:
            dk_s[:nk, :] += dk
            dv_s[:nk, :] += dv

    group_keys = seq_len // groups
    per_group = group_keys // rows
    for g in reversed(range(groups)):
        nk = (g + 1) * group_keys
        if g == groups - 1 and per_group > 1:
            dk_s[...] = jnp.zeros_like(dk_s)
            dv_s[...] = jnp.zeros_like(dv_s)
        first = g == groups - 1 and per_group == 1
        if per_group == 1:
            attend(g * group_keys, nk, group_keys, first)
        else:

            def step(j, carry, g=g, nk=nk):
                q0 = pl.multiple_of(g * group_keys + j * rows, rows)
                attend(q0, nk, group_keys, False)
                return carry

            lax.fori_loop(0, per_group, step, 0)

    def finish(j, carry):
        span = pl.ds(pl.multiple_of(j * rows, rows), rows)
        dproj_ref[span, 128:256] = rope(dk_s[span, :] * (1.0 / log2_e), span, True).astype(bf16)
        dproj_ref[span, 256:] = dv_s[span, :].astype(bf16)
        return carry

    lax.fori_loop(0, seq_len // rows, finish, 0)


def attention(length, attn_in, cot, w, bias, out_w, cos, sin_lo, sin_hi):
    seq_len = attn_in.shape[0]
    pairs = w.shape[1] // 384
    rows = 256
    groups = 6
    whole = functools.partial(pl.BlockSpec, pipeline_mode=pl.Buffered(1))
    small = pltpu.VMEM((seq_len, 128), bf16)
    turned = pltpu.VMEM((128, seq_len), bf16)
    wide = pltpu.VMEM((seq_len, 128), f32)
    flops = pairs * seq_len * (2 * D * 512 + 12 * 128 * seq_len)
    return pl.pallas_call(
        functools.partial(attention_kernel, seq_len=seq_len, rows=rows, groups=groups),
        grid=(pairs,),
        in_specs=[
            pl.BlockSpec(memory_space=pltpu.SMEM),
            whole((seq_len, D), lambda p: (0, 0)),
            whole((seq_len, D), lambda p: (0, 0)),
            pl.BlockSpec((D, 384), lambda p: (0, p)),
            pl.BlockSpec((1, 384), lambda p: (0, p)),
            pl.BlockSpec((128, D), lambda p: (p, 0)),
            whole((seq_len, 128), lambda p: (0, 0)),
            whole((seq_len, 128), lambda p: (0, 0)),
            whole((seq_len, 128), lambda p: (0, 0)),
        ],
        out_specs=[
            pl.BlockSpec((seq_len, 128), lambda p: (0, p)),
            pl.BlockSpec((seq_len, 384), lambda p: (0, p)),
        ],
        out_shape=[
            jax.ShapeDtypeStruct((seq_len, pairs * 128), bf16),
            jax.ShapeDtypeStruct((seq_len, pairs * 384), bf16),
        ],
        scratch_shapes=[small] * 5 + [turned] * 4 + [wide] * 3,
        compiler_params=pltpu.CompilerParams(vmem_limit_bytes=58 * 1024 * 1024),
        cost_estimate=pl.CostEstimate(
            flops=flops, bytes_accessed=12_000_000, transcendentals=pairs * seq_len * seq_len
        ),
        name="attention",
    )(length, attn_in, cot, w, bias, out_w, cos, sin_lo, sin_hi)


def swap(x, axis, by):
    n = lax.axis_size(axis)
    return lax.ppermute(x, axis, [(j, j ^ by) for j in range(n)])


def place(out, piece, at, axis=0):
    return lax.dynamic_update_slice_in_dim(out, piece, at * piece.shape[axis], axis)


def take(x, at, size, axis=0):
    return lax.dynamic_slice_in_dim(x, at * size, size, axis)


def gather(x, axis, me, n, step=1, dim=0):
    shape = list(x.shape)
    shape[dim] *= n
    out = place(jnp.zeros(shape, x.dtype), x, me, dim)
    for s in range(1, n):
        out = place(out, swap(x, axis, s * step), me ^ s, dim)
    return out


def scatter_sum(x, axis, me, n, step=1, dim=0):
    size = x.shape[dim] // n
    total = take(x, me, size, dim).astype(f32)
    for s in range(1, n):
        part = take(x, me ^ s, size, dim).astype(bf16)
        total = total + swap(part, axis, s * step).astype(f32)
    return total


def exchange(x, axis, me, n, step=1):
    out = place(jnp.zeros_like(x), take(x, me, 1), me)
    for s in range(1, n):
        out = place(out, swap(take(x, me ^ s, 1), axis, s * step), me ^ s)
    return out


def rope_tables(seq_len):
    half = ROTARY // 2
    frequency = rope_base ** (-2.0 * jnp.arange(half, dtype=f32) / ROTARY)
    angles = jnp.arange(seq_len, dtype=jnp.int32).astype(f32)[:, None] * frequency[None, :]
    cosine, sine = jnp.cos(angles), jnp.sin(angles)
    rest = jnp.zeros((seq_len, HEAD_DIM - ROTARY), f32)
    none = jnp.zeros((seq_len, half), f32)
    cos = jnp.concatenate([cosine, cosine, rest + 1.0] * 2, 1)
    sin_lo = jnp.concatenate([-sine, none, rest] * 2, 1)
    sin_hi = jnp.concatenate([none, sine, rest] * 2, 1)
    return cos, sin_lo, sin_hi


def local(
    tokens,
    lengths,
    cotangent,
    qkv_weight,
    qkv_bias,
    out_weight,
    out_bias,
    up_weight,
    up_bias,
    down_weight,
    down_bias,
    attn_gain,
    attn_shift,
    mlp_gain,
    mlp_shift,
):
    seqs, width = tokens.shape[0], tokens.shape[1]
    ctx_size, fsdp = lax.axis_size("ctx"), lax.axis_size("fsdp")
    team = ctx_size // seqs
    here = lax.axis_index("ctx")
    seat, seq = here % team, here // team
    shard = lax.axis_index("fsdp")
    seq_len = ctx_size * width
    heads = HEADS // team
    pairs = (heads + 1) // 2
    lanes = heads * HEAD_DIM
    spare = pairs * 128 - lanes

    def by_pair(x):
        rows = x.shape[0]
        x = take(x.reshape(rows, 3, D), seat, lanes, 2)
        x = jnp.pad(x, ((0, 0), (0, 0), (0, spare)))
        return jnp.concatenate(
            [x[:, t, p * 128 : (p + 1) * 128] for p in range(pairs) for t in range(3)], 1
        )

    def from_pair(x):
        rows = x.shape[0]
        parts = []
        for t in range(3):
            parts.append(
                jnp.concatenate(
                    [x[:, p * 384 + t * 128 : p * 384 + (t + 1) * 128] for p in range(pairs)], 1
                )[:, None, :lanes]
            )
        return jnp.concatenate(parts, 1).reshape(rows, 3, lanes)

    unit = FF // (fsdp * team)

    def up_columns(x):
        return jnp.concatenate(
            [take(x[:, j * unit * team : (j + 1) * unit * team], seat, unit, 1) for j in range(fsdp)],
            1,
        )

    tok_half = exchange(tokens, "ctx", seq, seqs, team)
    cot_half = exchange(cotangent, "ctx", seq, seqs, team)

    def join(half):
        return gather(half[:, None], "ctx", seat, team, 1, 1).reshape(seq_len, D)

    rows_in = join(tok_half)
    cot = join(cot_half)

    vectors = jnp.concatenate(
        [qkv_bias, out_bias, up_bias, down_bias, attn_gain, attn_shift, mlp_gain, mlp_shift]
    )[None]
    vectors = gather(vectors, "fsdp", shard, fsdp)
    bounds = []
    at = 0
    for v in (qkv_bias, out_bias, up_bias, down_bias, attn_gain, attn_shift, mlp_gain, mlp_shift):
        bounds.append(vectors[:, at : at + v.shape[0]].reshape(-1).astype(f32))
        at += v.shape[0]
    full_qkv_b, full_out_b, full_up_b, full_down_b, gain_a, shift_a, gain_m, shift_m = bounds
    w_up = gather(up_columns(up_weight), "fsdp", shard, fsdp)
    w_down = gather(take(down_weight, seat, unit), "fsdp", shard, fsdp)
    w_qkv = gather(by_pair(qkv_weight), "fsdp", shard, fsdp)
    w_out = gather(out_weight, "fsdp", shard, fsdp)
    w_out_rows = take(w_out, seat, lanes)
    w_out_rows = jnp.pad(w_out_rows, ((0, spare), (0, 0)))
    b_qkv = by_pair(full_qkv_b[None])
    b_up = up_columns(full_up_b[None])

    def normalise(x):
        x = x.astype(f32)
        center = x - jnp.mean(x, -1, keepdims=True)
        inv = lax.rsqrt(jnp.mean(center * center, -1, keepdims=True) + norm_eps)
        return center * inv, inv

    normed, _ = normalise(rows_in)
    attn_in = (normed * gain_a + shift_a).astype(bf16)
    mlp_in = (normed * gain_m + shift_m).astype(bf16)

    pre_act = dot(mlp_in, w_up) + b_up
    cdf = 0.5 * (1.0 + lax.erf(pre_act * inv_sqrt_two))
    hidden = (pre_act * cdf).astype(bf16)
    slope = cdf + pre_act * jnp.exp(-0.5 * pre_act * pre_act) * inv_sqrt_tau
    grad_pre = (dot(cot, w_down, NT) * slope).astype(bf16)
    down_grad = dot(hidden, cot, TN)
    up_grad = dot(mlp_in, grad_pre, TN)
    mlp_out = dot(hidden, w_down)
    grad_mlp_in = dot(grad_pre, w_up, NT)

    length = lax.dynamic_slice_in_dim(lengths, seq, 1, 0)
    mixed, grad_proj = attention(
        length, attn_in, cot, w_qkv, b_qkv, w_out_rows, *rope_tables(seq_len)
    )
    delta_out = mlp_out + dot(mixed, w_out_rows)
    mixed_all = gather(mixed[:, :lanes], "ctx", seat, team, 1, 1)
    out_cols = D // team
    out_grad = dot(mixed_all, take(cot, seat, out_cols, 1), TN)
    qkv_grad = dot(attn_in, grad_proj, TN)
    grad_attn_in = dot(grad_proj, w_qkv, NT)

    def home(x):
        blocks = x.reshape(seqs, team, width, D)
        return scatter_sum(blocks, "ctx", seat, team, 1, 1).reshape(seqs, width, D)

    delta_home = exchange(home(delta_out).astype(bf16), "ctx", seq, seqs, team)
    layer_out = (tokens.astype(f32) + delta_home.astype(f32) + full_out_b + full_down_b).astype(
        bf16
    )

    grad_normed = home(grad_attn_in * gain_a + grad_mlp_in * gain_m)
    normed_half, inv_half = normalise(tok_half)
    delta_in = inv_half * (
        grad_normed
        - jnp.mean(grad_normed, -1, keepdims=True)
        - normed_half * jnp.mean(grad_normed * normed_half, -1, keepdims=True)
    )
    delta_in = exchange(delta_in.astype(bf16), "ctx", seq, seqs, team)
    tokens_grad = cotangent.astype(f32) + delta_in.astype(f32)

    qkv_b_grad = from_pair(jnp.sum(grad_proj.astype(f32), 0)[None])
    qkv_b_grad = place(jnp.zeros((3, D), f32), qkv_b_grad[0], seat, 1)
    up_b_grad = jnp.sum(grad_pre.astype(f32), 0).reshape(fsdp, unit)
    up_b_grad = place(jnp.zeros((fsdp, unit * team), f32), up_b_grad, seat, 1)
    cot_sum = jnp.sum(cot.astype(f32), 0) * (1.0 / team)
    sums = [
        qkv_b_grad.reshape(-1),
        cot_sum,
        up_b_grad.reshape(-1),
        jnp.sum(grad_attn_in * normed, 0),
        jnp.sum(grad_attn_in, 0),
        jnp.sum(grad_mlp_in * normed, 0),
        jnp.sum(grad_mlp_in, 0),
    ]
    total = lax.psum(jnp.concatenate(sums).reshape(-1, 128), ("ctx", "fsdp")).reshape(-1)
    vec = []
    at = 0
    for v in sums:
        size = v.shape[0] // fsdp
        vec.append(lax.dynamic_slice_in_dim(total[at : at + v.shape[0]], shard * size, size, 0))
        at += v.shape[0]

    def reduce(x):
        mine = scatter_sum(x, "fsdp", shard, fsdp)
        part = scatter_sum(mine, "ctx", seq, seqs, team).astype(bf16)
        return gather(part, "ctx", seq, seqs, team)

    up_mine = reduce(up_grad).reshape(D // fsdp, fsdp, 1, unit)
    up_mine = gather(up_mine, "ctx", seat, team, 1, 2).reshape(D // fsdp, FF).astype(f32)
    down_mine = gather(reduce(down_grad), "ctx", seat, team).astype(f32)
    qkv_mine = from_pair(reduce(qkv_grad))
    qkv_mine = gather(qkv_mine, "ctx", seat, team, 1, 2).reshape(D // fsdp, 3 * D).astype(f32)
    out_mine = gather(reduce(out_grad), "ctx", seat, team, 1, 1).astype(f32)

    return (
        layer_out,
        tokens_grad,
        qkv_mine,
        vec[0],
        out_mine,
        vec[1],
        up_mine,
        vec[2],
        down_mine,
        vec[1],
        vec[3],
        vec[4],
        vec[5],
        vec[6],
    )


def solution(mesh):
    rows, whole = P("fsdp", "ctx", None), P("fsdp", None)
    vector = P("fsdp")
    in_specs = (
        rows,
        vector,
        rows,
        whole,
        vector,
        whole,
        vector,
        whole,
        vector,
        whole,
        vector,
        vector,
        vector,
        vector,
        vector,
    )
    out_specs = (
        rows,
        rows,
        whole,
        vector,
        whole,
        vector,
        whole,
        vector,
        whole,
        vector,
        vector,
        vector,
        vector,
        vector,
    )
    return jax.shard_map(local, mesh=mesh, in_specs=in_specs, out_specs=out_specs, check_vma=False)
```

```python
import functools
import math

import jax
import jax.numpy as jnp
import numpy as np
from jax import lax
from jax.experimental import pallas as pl
from jax.experimental.pallas import tpu as pltpu
from jax.sharding import PartitionSpec as P

D = 768
HEADS = 12
HEAD_DIM = 64
FF = 3072
ROTARY = 16

norm_eps = 1e-05
rope_base = 10000.0
inv_sqrt_two = 0.7071067811865476
inv_sqrt_tau = 0.3989422804014327
log2_e = 1.4426950408889634
masked_bias = -1e30
score_scale = HEAD_DIM ** (-0.5)

f32 = jnp.float32
bf16 = jnp.bfloat16
NT = (((1,), (1,)), ((), ()))
NN = (((1,), (0,)), ((), ()))
TN = (((0,), (0,)), ((), ()))


def dot(a, b, dims=NN):
    return lax.dot_general(a, b, dims, preferred_element_type=f32)


def attention_kernel(
    length_ref,
    attn_in_ref,
    cot_ref,
    w_ref,
    bias_ref,
    out_w_ref,
    cos_ref,
    sin_ref,
    mixed_ref,
    dproj_ref,
    q_s,
    k_a,
    k_b,
    v_a,
    v_b,
    kt_a,
    kt_b,
    vt_a,
    vt_b,
    do_s,
    dk_s,
    dv_s,
    *,
    seq_len,
    rows,
    groups,
):
    live = length_ref[0]
    lane = lax.broadcasted_iota(jnp.int32, (rows, 128), 1)
    low = lane < HEAD_DIM
    first_half = lane % HEAD_DIM < ROTARY // 2

    def rope(x, span, back):
        partner = jnp.where(first_half, pltpu.roll(x, 120, 1), pltpu.roll(x, 8, 1))
        partner = partner * sin_ref[span, :]
        turned = x * cos_ref[span, :]
        return turned - partner if back else turned + partner

    def project(j, carry):
        start = pl.multiple_of(j * rows, rows)
        span = pl.ds(start, rows)
        proj = dot(attn_in_ref[span, :], w_ref[...]) + bias_ref[...]
        q_s[span, :] = (rope(proj[:, :128], span, False) * (score_scale * log2_e)).astype(bf16)
        keys = rope(proj[:, 128:256], span, False)
        values = proj[:, 256:]
        key_pos = start + lax.broadcasted_iota(jnp.int32, (rows, 128), 0)
        dead = jnp.where(key_pos < live, 0.0, masked_bias)
        ka = jnp.where(low, keys, jnp.where(lane == HEAD_DIM, dead, 0.0))
        kb = jnp.where(low, jnp.where(lane == 0, dead, 0.0), keys)
        va = jnp.where(low, values, 1.0)
        vb = jnp.where(low, 1.0, values)
        for src, plain, turned in (
            (ka, k_a, kt_a),
            (kb, k_b, kt_b),
            (va, v_a, vt_a),
            (vb, v_b, vt_b),
        ):
            plain[span, :] = src.astype(bf16)
            turned[:, span] = src.T.astype(bf16)
        do_s[span, :] = dot(cot_ref[span, :], out_w_ref[...], NT)
        return carry

    lax.fori_loop(0, seq_len // rows, project, 0)

    def attend(q0, nk, group_keys, first):
        q_span = pl.ds(q0, rows)
        queries = q_s[q_span, :].astype(f32)
        zero = jnp.zeros_like(queries)
        qa = jnp.where(low, queries, zero).astype(bf16)
        qb = jnp.where(low, zero, queries).astype(bf16)
        qa1 = jnp.where(low, queries, jnp.where(lane == HEAD_DIM, 1.0, 0.0)).astype(bf16)
        qb1 = jnp.where(low, jnp.where(lane == 0, 1.0, 0.0), queries).astype(bf16)
        edge = nk - group_keys
        key_pos = edge + lax.broadcasted_iota(jnp.int32, (group_keys, rows), 0)
        query_pos = q0 + lax.broadcasted_iota(jnp.int32, (group_keys, rows), 1)
        causal = key_pos <= query_pos
        probs = []
        mixes = []
        for keys, turned, q1 in ((k_a, vt_a, qa1), (k_b, vt_b, qb1)):
            s_edge = dot(keys[edge:nk, :], q1, NT)
            s_edge = jnp.where(causal, s_edge, masked_bias)
            best = jnp.max(s_edge, 0, keepdims=True)
            if edge:
                s_body = dot(keys[:edge, :], q1, NT)
                best = jnp.maximum(best, jnp.max(s_body, 0, keepdims=True))
                p = jnp.concatenate(
                    [
                        jnp.exp2(s_body - best).astype(bf16),
                        jnp.exp2(s_edge - best).astype(bf16),
                    ],
                    0,
                )
            else:
                p = jnp.exp2(s_edge - best).astype(bf16)
            probs.append(p)
            mixes.append(dot(turned[:, :nk], p).T)
        unscaled = jnp.where(low, mixes[0], mixes[1])
        denom = pltpu.roll(jnp.where(low, mixes[1], mixes[0]), HEAD_DIM, 1)
        inv = 1.0 / denom
        out = unscaled * inv
        mixed_ref[q_span, :] = out.astype(bf16)
        grad = (do_s[q_span, :] * inv).astype(bf16)
        grad_f = grad.astype(f32)
        prod = grad_f * out
        da = jnp.sum(jnp.where(low, prod, 0.0), 1, keepdims=True)
        db = jnp.sum(jnp.where(low, 0.0, prod), 1, keepdims=True)
        da_hi = da.astype(bf16).astype(f32)
        db_hi = db.astype(bf16).astype(f32)
        ga = jnp.where(low, grad_f, 0.0)
        gb = jnp.where(low, 0.0, grad_f)
        ga1 = jnp.where(
            lane == HEAD_DIM, -da_hi, jnp.where(lane == HEAD_DIM + 1, da_hi - da, ga)
        ).astype(bf16)
        gb1 = jnp.where(lane == 0, -db_hi, jnp.where(lane == 1, db_hi - db, gb)).astype(bf16)
        ga = ga.astype(bf16)
        gb = gb.astype(bf16)
        grad_scores = []
        for p, values, g1 in zip(probs, (v_a, v_b), (ga1, gb1)):
            dp = dot(values[:nk, :], g1, NT)
            grad_scores.append((p.astype(f32) * dp).astype(bf16))
        dq = dot(kt_a[:, :nk], grad_scores[0]) + dot(kt_b[:, :nk], grad_scores[1])
        dproj_ref[q_span, :128] = rope(dq.T * score_scale, q_span, True).astype(bf16)
        dk = dot(jnp.concatenate(grad_scores, 1), jnp.concatenate([qa, qb], 0))
        dv = dot(jnp.concatenate(probs, 1), jnp.concatenate([ga, gb], 0))
        if first:
            dk_s[:nk, :] = dk
            dv_s[:nk, :] = dv
        else:
            dk_s[:nk, :] += dk
            dv_s[:nk, :] += dv

    group_keys = seq_len // groups
    per_group = group_keys // rows
    for g in reversed(range(groups)):
        nk = (g + 1) * group_keys
        if g == groups - 1 and per_group > 1:
            dk_s[...] = jnp.zeros_like(dk_s)
            dv_s[...] = jnp.zeros_like(dv_s)
        first = g == groups - 1 and per_group == 1
        if per_group == 1:
            attend(g * group_keys, nk, group_keys, first)
        else:

            def step(j, carry, g=g, nk=nk):
                q0 = pl.multiple_of(g * group_keys + j * rows, rows)
                attend(q0, nk, group_keys, False)
                return carry

            lax.fori_loop(0, per_group, step, 0)

    def finish(j, carry):
        span = pl.ds(pl.multiple_of(j * rows, rows), rows)
        dproj_ref[span, 128:256] = rope(dk_s[span, :] * (1.0 / log2_e), span, True).astype(bf16)
        dproj_ref[span, 256:] = dv_s[span, :].astype(bf16)
        return carry

    lax.fori_loop(0, seq_len // rows, finish, 0)


def attention(length, attn_in, cot, w, bias, out_w, cos, sin):
    seq_len = attn_in.shape[0]
    pairs = w.shape[1] // 384
    rows = 256
    groups = 6
    whole = functools.partial(pl.BlockSpec, pipeline_mode=pl.Buffered(1))
    small = pltpu.VMEM((seq_len, 128), bf16)
    turned = pltpu.VMEM((128, seq_len), bf16)
    wide = pltpu.VMEM((seq_len, 128), f32)
    flops = pairs * seq_len * (2 * D * 512 + 12 * 128 * seq_len)
    return pl.pallas_call(
        functools.partial(attention_kernel, seq_len=seq_len, rows=rows, groups=groups),
        grid=(pairs,),
        in_specs=[
            pl.BlockSpec(memory_space=pltpu.SMEM),
            whole((seq_len, D), lambda p: (0, 0)),
            whole((seq_len, D), lambda p: (0, 0)),
            pl.BlockSpec((D, 384), lambda p: (0, p)),
            pl.BlockSpec((1, 384), lambda p: (0, p)),
            pl.BlockSpec((128, D), lambda p: (p, 0)),
            whole((seq_len, 128), lambda p: (0, 0)),
            whole((seq_len, 128), lambda p: (0, 0)),
        ],
        out_specs=[
            pl.BlockSpec((seq_len, 128), lambda p: (0, p)),
            pl.BlockSpec((seq_len, 384), lambda p: (0, p)),
        ],
        out_shape=[
            jax.ShapeDtypeStruct((seq_len, pairs * 128), bf16),
            jax.ShapeDtypeStruct((seq_len, pairs * 384), bf16),
        ],
        scratch_shapes=[small] * 5 + [turned] * 4 + [wide] * 3,
        compiler_params=pltpu.CompilerParams(vmem_limit_bytes=58 * 1024 * 1024),
        cost_estimate=pl.CostEstimate(
            flops=flops, bytes_accessed=12_000_000, transcendentals=pairs * seq_len * seq_len
        ),
        name="attention",
    )(length, attn_in, cot, w, bias, out_w, cos, sin)


def mlp_kernel(
    shard_ref,
    rows_ref,
    cot_ref,
    affine_ref,
    bias_ref,
    *refs,
    layout,
    fsdp,
    own_rows,
    unit,
    chunk,
):
    pieces = refs[: len(layout)]
    attn_in_ref, out_ref, grad_in_ref, grads_ref, vec_ref = refs[len(layout) : len(layout) + 5]
    mlp_in, mlp_in_t, w_up, w_down, sems = refs[len(layout) + 5 :]
    seq_len = rows_ref.shape[0]
    up_width = fsdp * unit
    folds = unit // own_rows
    rows = 256

    copies = []
    for n, (k, first, count) in enumerate(layout):
        j = shard_ref[0] ^ k
        count = min(count, own_rows - first)
        source = pl.ds(0, count)
        at = pl.ds(pl.multiple_of(j * own_rows + first, 16), count)
        copies.append(
            pltpu.make_async_copy(
                pieces[n].at[source, pl.ds(0, up_width)], w_up.at[at, :], sems.at[n, 0]
            )
        )
        for i in range(folds):
            at = pl.ds(pl.multiple_of(j * unit + i * own_rows + first, 16), count)
            copies.append(
                pltpu.make_async_copy(
                    pieces[n].at[source, pl.ds(up_width + i * D, D)],
                    w_down.at[at, :],
                    sems.at[n, 1 + i],
                )
            )
    for copy in copies:
        copy.start()

    def normed_rows(span):
        x = rows_ref[span, :].astype(f32)
        center = x - jnp.mean(x, -1, keepdims=True)
        return center * lax.rsqrt(jnp.mean(center * center, -1, keepdims=True) + norm_eps)

    def prepare(j, cot_sum):
        span = pl.ds(pl.multiple_of(j * rows, rows), rows)
        normed = normed_rows(span)
        attn_in_ref[span, :] = (normed * affine_ref[0:1, :] + affine_ref[1:2, :]).astype(bf16)
        scaled = normed * affine_ref[2:3, :] + affine_ref[3:4, :]
        mlp_in[span, :] = scaled.astype(bf16)
        mlp_in_t[:, span] = scaled.T.astype(bf16)
        return cot_sum + jnp.sum(cot_ref[span, :].astype(f32), 0, keepdims=True)

    cot_sum = lax.fori_loop(0, seq_len // rows, prepare, jnp.zeros((1, D), f32))
    for copy in copies:
        copy.wait()

    for c in range(up_width // chunk):
        part = slice(c * chunk, (c + 1) * chunk)
        pre_act = dot(mlp_in[...], w_up[:, part]) + bias_ref[:, part]
        cdf = 0.5 + 0.5 * lax.erf(pre_act * inv_sqrt_two)
        hidden = (pre_act * cdf).astype(bf16)
        slope = cdf + pre_act * jnp.exp(-0.5 * pre_act * pre_act) * inv_sqrt_tau
        grad_pre = (dot(cot_ref[...], w_down[part, :], NT) * slope).astype(bf16)
        vec_ref[0:1, part] = jnp.sum(grad_pre.astype(f32), 0, keepdims=True)
        forward = dot(hidden, w_down[part, :])
        backward = dot(grad_pre, w_up[:, part], NT)
        if c == 0:
            out_ref[...] = forward
            grad_in_ref[...] = backward
        else:
            out_ref[...] += forward
            grad_in_ref[...] += backward
        up_grad = dot(mlp_in_t[...], grad_pre).astype(bf16)
        for j in range(fsdp):
            grads_ref[j, :own_rows, part] = up_grad[j * own_rows : (j + 1) * own_rows]
        down_grad = dot(hidden, cot_ref[...], TN).astype(bf16)
        step = math.gcd(own_rows, chunk)
        for r in range(0, chunk, step):
            u = c * chunk + r
            j, i, at = u // unit, u % unit // own_rows, u % own_rows
            grads_ref[j, at : at + step, up_width + i * D : up_width + (i + 1) * D] = down_grad[
                r : r + step
            ]

    def sums(j, carry):
        span = pl.ds(pl.multiple_of(j * rows, rows), rows)
        grad = grad_in_ref[span, :]
        return (
            carry[0] + jnp.sum(grad * normed_rows(span), 0, keepdims=True),
            carry[1] + jnp.sum(grad, 0, keepdims=True),
        )

    none = jnp.zeros((1, D), f32)
    gain_sum, shift_sum = lax.fori_loop(0, seq_len // rows, sums, (none, none))
    vec_ref[1:2, :D] = gain_sum
    vec_ref[2:3, :D] = shift_sum
    vec_ref[3:4, :D] = cot_sum


def mlp(shard, rows_in, cot, affine, bias, got, fsdp, unit):
    seq_len = rows_in.shape[0]
    layout = [(k, first, piece.shape[0]) for k, first, piece in got]
    pieces = [piece for _, _, piece in got]
    own_rows = D // fsdp
    packed_width = pieces[0].shape[1]
    up_width = fsdp * unit
    chunk = 256
    vmem = pl.BlockSpec(memory_space=pltpu.VMEM)
    return pl.pallas_call(
        functools.partial(
            mlp_kernel, layout=layout, fsdp=fsdp, own_rows=own_rows, unit=unit, chunk=chunk
        ),
        in_specs=[pl.BlockSpec(memory_space=pltpu.SMEM)]
        + [vmem] * 4
        + [pl.BlockSpec(memory_space=pl.ANY)] * len(pieces),
        out_specs=[vmem] * 5,
        out_shape=[
            jax.ShapeDtypeStruct((seq_len, D), bf16),
            jax.ShapeDtypeStruct((seq_len, D), f32),
            jax.ShapeDtypeStruct((seq_len, D), f32),
            jax.ShapeDtypeStruct((fsdp, own_rows + 16, packed_width), bf16),
            jax.ShapeDtypeStruct((8, up_width), f32),
        ],
        scratch_shapes=[
            pltpu.VMEM((seq_len, D), bf16),
            pltpu.VMEM((D, seq_len), bf16),
            pltpu.VMEM((D, up_width), bf16),
            pltpu.VMEM((up_width, D), bf16),
            pltpu.SemaphoreType.DMA((len(pieces), 1 + unit // own_rows)),
        ],
        compiler_params=pltpu.CompilerParams(vmem_limit_bytes=58 * 1024 * 1024),
        cost_estimate=pl.CostEstimate(
            flops=12 * seq_len * D * up_width,
            bytes_accessed=30_000_000,
            transcendentals=2 * seq_len * up_width,
        ),
        name="mlp",
    )(shard, rows_in, cot, affine, bias, *pieces)


def take(x, at, size, axis=0):
    return lax.dynamic_slice_in_dim(x, at * size, size, axis)


def place(out, piece, at, axis=0):
    return lax.dynamic_update_slice_in_dim(out, piece, at * piece.shape[axis], axis)


def swap(x, axis, by):
    n = lax.axis_size(axis)
    return lax.ppermute(x, axis, [(j, j ^ by) for j in range(n)])


def exchange(x, group):
    axis, n, step, me = group
    return [(me ^ s, swap(take(x, me ^ s, 1), axis, s * step) if s else take(x, me, 1)) for s in range(n)]


def gather(x, group):
    axis, n, step, me = group
    return [(me ^ s, swap(x, axis, s * step) if s else x) for s in range(n)]


def gather_rows(x, group):
    axis, n, step, _ = group
    if n != 4:
        return [(k, 0, swap(x, axis, k * step) if k else x) for k in range(n)]
    one, two = swap(x, axis, step), swap(x, axis, 2 * step)
    half = x.shape[0] // 2
    return [
        (0, 0, x),
        (1, 0, one),
        (2, 0, two),
        (3, 0, swap(one[:half], axis, 2 * step)),
        (3, half, swap(two[half:], axis, step)),
    ]


def stacked(pieces):
    if len(pieces) == 2:
        (me, own), (_, other) = pieces
        first = me == 0
        return jnp.stack([jnp.where(first, own, other), jnp.where(first, other, own)])
    out = jnp.zeros((len(pieces),) + pieces[0][1].shape, pieces[0][1].dtype)
    for j, piece in pieces:
        out = place(out, piece[None], j)
    return out


def after(x, pieces):
    held, arrived = lax.optimization_barrier((x, [piece[-1] for piece in pieces]))
    return held, [piece[:-1] + (got,) for piece, got in zip(pieces, arrived)]


def total(pieces):
    return sum(piece[0].astype(f32) for _, piece in pieces)


def scatter_sum(x, group):
    return total(exchange(x, group))


def rope_tables(seq_len):
    half = ROTARY // 2
    frequency = rope_base ** (-2.0 * np.arange(half) / ROTARY)
    angles = np.arange(seq_len)[:, None] * frequency[None, :]
    cosine, sine = np.cos(angles), np.sin(angles)
    rest = np.zeros((seq_len, HEAD_DIM - ROTARY))
    cos = np.concatenate([cosine, cosine, rest + 1.0] * 2, 1)
    sin = np.concatenate([-sine, sine, rest] * 2, 1)
    return jnp.asarray(cos, f32), jnp.asarray(sin, f32)


def local(
    tokens,
    lengths,
    cotangent,
    qkv_weight,
    qkv_bias,
    out_weight,
    out_bias,
    up_weight,
    up_bias,
    down_weight,
    down_bias,
    attn_gain,
    attn_shift,
    mlp_gain,
    mlp_shift,
):
    seqs, width = tokens.shape[0], tokens.shape[1]
    ctx_size, fsdp = lax.axis_size("ctx"), lax.axis_size("fsdp")
    team = ctx_size // seqs
    here = lax.axis_index("ctx")
    seat, seq = here % team, here // team
    shard = lax.axis_index("fsdp")
    seq_len = ctx_size * width
    heads = HEADS // team
    pairs = (heads + 1) // 2
    lanes = heads * HEAD_DIM
    spare = pairs * 128 - lanes

    def by_pair(x):
        rows = x.shape[0]
        x = take(x.reshape(rows, 3, D), seat, lanes, 2)
        x = jnp.pad(x, ((0, 0), (0, 0), (0, spare)))
        return jnp.concatenate(
            [x[:, t, p * 128 : (p + 1) * 128] for p in range(pairs) for t in range(3)], 1
        )

    unit = FF // (fsdp * team)

    def up_columns(x):
        return jnp.concatenate(
            [take(x[:, j * unit * team : (j + 1) * unit * team], seat, unit, 1) for j in range(fsdp)],
            1,
        )

    seqs_group = ("ctx", seqs, team, seq)
    team_group = ("ctx", team, 1, seat)
    fsdp_group = ("fsdp", fsdp, 1, shard)
    own_rows = D // fsdp
    folds = unit // own_rows

    both = []
    for s in range(seqs):
        block = jnp.concatenate([take(tokens, seq ^ s, 1), take(cotangent, seq ^ s, 1)])
        both.append((seq ^ s, swap(block, "ctx", s * team) if s else block))
    half = stacked(both)
    joined = gather(half, team_group)
    tok_half = half[:, 0]
    rows_in = stacked([(j, h[:, 0]) for j, h in joined]).swapaxes(0, 1).reshape(seq_len, D)
    cot = stacked([(j, h[:, 1]) for j, h in joined]).swapaxes(0, 1).reshape(seq_len, D)

    down_own = take(down_weight, seat, unit)
    mlp_pack = jnp.concatenate(
        [up_columns(up_weight)] + [down_own[i * own_rows : (i + 1) * own_rows] for i in range(folds)],
        1,
    )
    up_width = fsdp * unit
    mlp_width = up_width + folds * D
    vectors = (qkv_bias, out_bias, up_bias, down_bias, attn_gain, attn_shift, mlp_gain, mlp_shift)
    vector_size = sum(v.shape[0] for v in vectors)
    vector_pack = jnp.pad(jnp.concatenate(vectors), (0, mlp_width - vector_size))
    vector_pack = jnp.pad(vector_pack[None], ((0, 31), (0, 0)))
    mlp_pack = jnp.concatenate([mlp_pack, vector_pack], 0)
    mlp_got = gather_rows(mlp_pack, fsdp_group)
    attn_pack = jnp.concatenate([by_pair(qkv_weight), out_weight], 1)
    attn_pack, mlp_got = after(attn_pack, mlp_got)
    attn_got = gather_rows(attn_pack, fsdp_group)
    qkv_width = pairs * 384
    packed = stacked(
        [
            (shard ^ k, piece[own_rows - first, :vector_size])
            for k, first, piece in mlp_got
            if first <= own_rows < first + piece.shape[0]
        ]
    )
    bounds = []
    at = 0
    for v in vectors:
        bounds.append(packed[:, at : at + v.shape[0]].reshape(-1).astype(f32))
        at += v.shape[0]
    full_qkv_b, full_out_b, full_up_b, full_down_b, gain_a, shift_a, gain_m, shift_m = bounds
    w_qkv = jnp.zeros((D, qkv_width), bf16)
    w_out = jnp.zeros((D, D), bf16)
    for k, first, piece in attn_got:
        at = (shard ^ k) * own_rows + first
        w_qkv = lax.dynamic_update_slice(w_qkv, piece[:, :qkv_width], (at, 0))
        w_out = lax.dynamic_update_slice(w_out, piece[:, qkv_width:], (at, 0))
    w_out_rows = jnp.pad(take(w_out, seat, lanes), ((0, spare), (0, 0)))
    b_qkv = by_pair(full_qkv_b[None])
    b_up = up_columns(full_up_b[None])

    def normalise(x):
        x = x.astype(f32)
        center = x - jnp.mean(x, -1, keepdims=True)
        inv = lax.rsqrt(jnp.mean(center * center, -1, keepdims=True) + norm_eps)
        return center * inv, inv

    def columns(x):
        return jnp.sum(x, 0)

    def vector_row(parts, size):
        row = jnp.concatenate([v.reshape(fsdp, -1) for v in parts], 1)
        row = jnp.pad(row, ((0, 0), (0, size - row.shape[1])))[:, None]
        return jnp.pad(row, ((0, 0), (0, 15), (0, 0))).astype(bf16)

    normed, _ = normalise(rows_in)
    if seq_len <= 2048:
        affine = jnp.concatenate(
            [gain_a[None], shift_a[None], gain_m[None], shift_m[None], jnp.zeros((4, D), f32)]
        )
        attn_in, mlp_out, grad_mlp_in, mlp_grads, sums = mlp(
            shard.reshape(1).astype(jnp.int32),
            rows_in,
            cot,
            affine,
            b_up,
            mlp_got,
            fsdp,
            unit,
        )
        row = vector_row(
            [sums[0], sums[1, :D], sums[2, :D], sums[3, :D] * (1.0 / team)], mlp_width
        )
        mlp_grads = lax.dynamic_update_slice(mlp_grads, row, (0, own_rows, 0))
    else:
        w_up = jnp.zeros((D, up_width), bf16)
        w_down = jnp.zeros((fsdp, folds, own_rows, D), bf16)
        for k, _, piece in mlp_got:
            w_up = place(w_up, piece[:own_rows, :up_width], shard ^ k)
            for i in range(folds):
                part = piece[:own_rows, up_width + i * D : up_width + (i + 1) * D]
                w_down = lax.dynamic_update_slice(w_down, part[None, None], (shard ^ k, i, 0, 0))
        w_down = w_down.reshape(up_width, D)
        attn_in = (normed * gain_a + shift_a).astype(bf16)
        mlp_in = (normed * gain_m + shift_m).astype(bf16)

        pre_act = dot(mlp_in, w_up) + b_up
        cdf = 0.5 * (1.0 + lax.erf(pre_act * inv_sqrt_two))
        hidden = (pre_act * cdf).astype(bf16)
        slope = cdf + pre_act * jnp.exp(-0.5 * pre_act * pre_act) * inv_sqrt_tau
        grad_pre = (dot(cot, w_down, NT) * slope).astype(bf16)
        down_grad = dot(hidden, cot, TN)
        up_grad = dot(mlp_in, grad_pre, TN)
        mlp_out = dot(hidden, w_down)
        grad_mlp_in = dot(grad_pre, w_up, NT)

        cot_sum = columns(cot.astype(f32)) * (1.0 / team)
        mlp_grads = jnp.concatenate(
            [up_grad.astype(bf16).reshape(fsdp, own_rows, up_width)]
            + [
                down_grad.astype(bf16).reshape(fsdp, folds, own_rows, D)[:, i] for i in range(folds)
            ],
            2,
        )
        mlp_grads = jnp.concatenate(
            [
                mlp_grads,
                vector_row(
                    [
                        columns(grad_pre.astype(f32)),
                        columns(grad_mlp_in * normed),
                        columns(grad_mlp_in),
                        cot_sum,
                    ],
                    mlp_width,
                ),
            ],
            1,
        )

    def spread(mine):
        cols = mine.shape[1] // seqs
        return [
            (s, swap(take(mine, seq ^ s, cols, 1), "ctx", s * team) if s else take(mine, seq, cols, 1))
            for s in range(seqs)
        ]

    def joined_columns(pieces):
        rows, cols = pieces[0][1].shape
        whole = jnp.zeros((rows, seqs * cols), bf16)
        for j, piece in pieces:
            whole = place(whole, piece, j, 1)
        return stacked(gather(whole, team_group))

    def summed(parts):
        return sum(part.astype(f32) for _, part in parts).astype(bf16)

    attn_in, cot_held, mlp_grads = lax.optimization_barrier((attn_in, cot, mlp_grads))
    mlp_pieces = exchange(mlp_grads, fsdp_group)
    length = lax.dynamic_slice_in_dim(lengths, seq, 1, 0)
    mixed, grad_proj = attention(
        length, attn_in, cot_held, w_qkv, b_qkv, w_out_rows, *rope_tables(seq_len)
    )
    (mixed, grad_proj), mlp_pieces = after((mixed, grad_proj), mlp_pieces)
    mlp_mine = total(mlp_pieces).astype(bf16)
    mixed, grad_proj, mlp_mine = lax.optimization_barrier((mixed, grad_proj, mlp_mine))
    mlp_parts = spread(mlp_mine)
    mixed_all = stacked(gather(mixed[:, :lanes], team_group)).swapaxes(0, 1).reshape(seq_len, D)
    qkv_grad = dot(attn_in, grad_proj, TN)
    grad_attn_in = dot(grad_proj, w_qkv, NT)
    delta_out = mlp_out + dot(mixed, w_out_rows)
    out_cols = D // team
    out_grad = dot(mixed_all, take(cot, seat, out_cols, 1), TN)

    qkv_b_grad = columns(grad_proj.astype(f32))
    qkv_b_grad = jnp.concatenate(
        [
            jnp.concatenate(
                [
                    qkv_b_grad[p * 384 + i * 128 : p * 384 + i * 128 + min(128, lanes - p * 128)]
                    for p in range(pairs)
                ]
            )[None]
            for i in range(3)
        ],
        0,
    )
    qkv_b_grad = place(jnp.zeros((3, D), f32), qkv_b_grad, seat, 1)
    attn_width = qkv_width + out_cols
    attn_grads = jnp.concatenate(
        [
            qkv_grad.astype(bf16).reshape(fsdp, own_rows, qkv_width),
            out_grad.astype(bf16).reshape(fsdp, own_rows, out_cols),
        ],
        2,
    )
    attn_grads = jnp.concatenate(
        [
            attn_grads,
            vector_row(
                [qkv_b_grad, columns(grad_attn_in * normed), columns(grad_attn_in)], attn_width
            ),
        ],
        1,
    )
    attn_pieces = exchange(attn_grads, fsdp_group)

    def home(x):
        return scatter_sum(x.astype(bf16).reshape(seqs, team, width, D).swapaxes(0, 1), team_group)

    def returned(pieces):
        return stacked([(j, piece[0]) for j, piece in pieces])

    delta_out, mlp_parts = after(home(delta_out).astype(bf16), mlp_parts)
    mlp_part = summed(mlp_parts)
    out_pieces = exchange(delta_out, seqs_group)

    grad_normed = home(grad_attn_in * gain_a + grad_mlp_in * gain_m)
    normed_half, inv_half = normalise(tok_half)
    delta_in = inv_half * (
        grad_normed
        - jnp.mean(grad_normed, -1, keepdims=True)
        - normed_half * jnp.mean(grad_normed * normed_half, -1, keepdims=True)
    )
    delta_in, out_pieces = after(delta_in.astype(bf16), out_pieces)
    in_pieces = exchange(delta_in, seqs_group)
    layer_out = (
        tokens.astype(f32) + returned(out_pieces).astype(f32) + full_out_b + full_down_b
    ).astype(bf16)

    mlp_part, in_pieces = after(mlp_part, in_pieces)
    tokens_grad = cotangent.astype(f32) + returned(in_pieces).astype(f32)
    mlp_whole = gather(mlp_part, seqs_group)
    attn_mine, mlp_whole = after(total(attn_pieces).astype(bf16), mlp_whole)
    attn_parts = spread(attn_mine)
    mlp_all = joined_columns(mlp_whole)
    attn_all = joined_columns(gather(summed(attn_parts), seqs_group))

    up_mine = jnp.concatenate(
        [
            mlp_all[t, :own_rows, j * unit : (j + 1) * unit]
            for j in range(fsdp)
            for t in range(team)
        ],
        1,
    ).astype(f32)
    down_mine = jnp.concatenate(
        [
            mlp_all[t, :own_rows, up_width + i * D : up_width + (i + 1) * D]
            for t in range(team)
            for i in range(folds)
        ],
        0,
    ).astype(f32)
    qkv_mine = jnp.concatenate(
        [
            attn_all[
                t, :own_rows, p * 384 + i * 128 : p * 384 + i * 128 + min(128, lanes - p * 128)
            ]
            for i in range(3)
            for t in range(team)
            for p in range(pairs)
        ],
        1,
    ).astype(f32)
    out_mine = jnp.concatenate([attn_all[t, :own_rows, qkv_width:] for t in range(team)], 1).astype(f32)
    mlp_vec = mlp_all[:, own_rows].astype(f32)
    attn_vec = columns(attn_all[:, own_rows].astype(f32))
    up_b_mine = mlp_vec[:, :unit].reshape(-1)
    mlp_vec = columns(mlp_vec)[unit:]
    bias_mine = mlp_vec[2 * own_rows : 3 * own_rows]
    qkv_b_mine = attn_vec[: 3 * own_rows]
    attn_vec = attn_vec[3 * own_rows :]

    return (
        layer_out,
        tokens_grad,
        qkv_mine,
        qkv_b_mine,
        out_mine,
        bias_mine,
        up_mine,
        up_b_mine,
        down_mine,
        bias_mine,
        attn_vec[:own_rows],
        attn_vec[own_rows : 2 * own_rows],
        mlp_vec[:own_rows],
        mlp_vec[own_rows : 2 * own_rows],
    )


def solution(mesh):
    rows, whole = P("fsdp", "ctx", None), P("fsdp", None)
    vector = P("fsdp")
    in_specs = (
        rows,
        vector,
        rows,
        whole,
        vector,
        whole,
        vector,
        whole,
        vector,
        whole,
        vector,
        vector,
        vector,
        vector,
        vector,
    )
    out_specs = (
        rows,
        rows,
        whole,
        vector,
        whole,
        vector,
        whole,
        vector,
        whole,
        vector,
        vector,
        vector,
        vector,
        vector,
    )
    return jax.shard_map(local, mesh=mesh, in_specs=in_specs, out_specs=out_specs, check_vma=False)
```

```python
import functools
import math

import jax
import jax.numpy as jnp
import numpy as np
from jax import lax
from jax.experimental import pallas as pl
from jax.experimental.pallas import tpu as pltpu
from jax.sharding import PartitionSpec as P

D = 768
HEADS = 12
HEAD_DIM = 64
FF = 3072
ROTARY = 16

norm_eps = 1e-05
rope_base = 10000.0
inv_sqrt_two = 0.7071067811865476
inv_sqrt_tau = 0.3989422804014327
log2_e = 1.4426950408889634
masked_bias = -1e30
score_scale = HEAD_DIM ** (-0.5)

f32 = jnp.float32
bf16 = jnp.bfloat16
NT = (((1,), (1,)), ((), ()))
NN = (((1,), (0,)), ((), ()))
TN = (((0,), (0,)), ((), ()))


def dot(a, b, dims=NN):
    return lax.dot_general(a, b, dims, preferred_element_type=f32)


def attention_kernel(
    scalar_ref,
    attn_in_ref,
    cot_ref,
    bias_ref,
    cos_ref,
    sin_ref,
    *refs,
    seq_len,
    rows,
    groups,
    fsdp,
    lanes,
):
    pieces, refs = refs[:fsdp], refs[fsdp:]
    mixed_ref, dproj_ref, w_s, out_w_s, sems = refs[:5]
    scratch = refs[5:]
    q_s, k_a, k_b, v_a, v_b, kt_a, kt_b, vt_a, vt_b, do_s, dk_s, dv_s = scratch
    pair = pl.program_id(0)
    own_rows = D // fsdp
    width = w_s.shape[1]

    @pl.when(pair == 0)
    def _():
        out_w_s[D:, :] = jnp.zeros((128, D), bf16)
        copies = []
        for k in range(fsdp):
            at = pl.ds(pl.multiple_of((scalar_ref[1] ^ k) * own_rows, own_rows), own_rows)
            copies.append(
                pltpu.make_async_copy(
                    pieces[k].at[:, pl.ds(0, width)], w_s.at[at, :], sems.at[k, 0]
                )
            )
            copies.append(
                pltpu.make_async_copy(
                    pieces[k].at[:, pl.ds(width, D)], out_w_s.at[at, :], sems.at[k, 1]
                )
            )
        for copy in copies:
            copy.start()
        for copy in copies:
            copy.wait()

    w_cols = pl.ds(pl.multiple_of(pair * 384, 128), 384)
    out_rows = pl.ds(pl.multiple_of(scalar_ref[2] * lanes + pair * 128, HEAD_DIM), 128)
    live = scalar_ref[0]
    lane = lax.broadcasted_iota(jnp.int32, (rows, 128), 1)
    low = lane < HEAD_DIM
    first_half = lane % HEAD_DIM < ROTARY // 2

    def rope(x, span, back):
        partner = jnp.where(first_half, pltpu.roll(x, 120, 1), pltpu.roll(x, 8, 1))
        partner = partner * sin_ref[span, :]
        turned = x * cos_ref[span, :]
        return turned - partner if back else turned + partner

    def project(j, carry):
        start = pl.multiple_of(j * rows, rows)
        span = pl.ds(start, rows)
        proj = dot(attn_in_ref[span, :], w_s[:, w_cols]) + bias_ref[...]
        q_s[span, :] = (rope(proj[:, :128], span, False) * (score_scale * log2_e)).astype(bf16)
        keys = rope(proj[:, 128:256], span, False)
        values = proj[:, 256:]
        key_pos = start + lax.broadcasted_iota(jnp.int32, (rows, 128), 0)
        dead = jnp.where(key_pos < live, 0.0, masked_bias)
        ka = jnp.where(low, keys, jnp.where(lane == HEAD_DIM, dead, 0.0))
        kb = jnp.where(low, jnp.where(lane == 0, dead, 0.0), keys)
        va = jnp.where(low, values, 1.0)
        vb = jnp.where(low, 1.0, values)
        for src, plain, turned in (
            (ka, k_a, kt_a),
            (kb, k_b, kt_b),
            (va, v_a, vt_a),
            (vb, v_b, vt_b),
        ):
            plain[span, :] = src.astype(bf16)
            turned[:, span] = src.T.astype(bf16)
        do_s[span, :] = dot(cot_ref[span, :], out_w_s[out_rows, :], NT)
        return carry

    lax.fori_loop(0, seq_len // rows, project, 0)

    def attend(q0, nk, group_keys, first):
        q_span = pl.ds(q0, rows)
        queries = q_s[q_span, :].astype(f32)
        zero = jnp.zeros_like(queries)
        qa = jnp.where(low, queries, zero).astype(bf16)
        qb = jnp.where(low, zero, queries).astype(bf16)
        qa1 = jnp.where(low, queries, jnp.where(lane == HEAD_DIM, 1.0, 0.0)).astype(bf16)
        qb1 = jnp.where(low, jnp.where(lane == 0, 1.0, 0.0), queries).astype(bf16)
        edge = nk - group_keys
        key_pos = edge + lax.broadcasted_iota(jnp.int32, (group_keys, rows), 0)
        query_pos = q0 + lax.broadcasted_iota(jnp.int32, (group_keys, rows), 1)
        causal = key_pos <= query_pos
        probs = []
        mixes = []
        for keys, turned, q1 in ((k_a, vt_a, qa1), (k_b, vt_b, qb1)):
            s_edge = dot(keys[edge:nk, :], q1, NT)
            s_edge = jnp.where(causal, s_edge, masked_bias)
            best = jnp.max(s_edge, 0, keepdims=True)
            if edge:
                s_body = dot(keys[:edge, :], q1, NT)
                best = jnp.maximum(best, jnp.max(s_body, 0, keepdims=True))
                p = jnp.concatenate(
                    [
                        jnp.exp2(s_body - best).astype(bf16),
                        jnp.exp2(s_edge - best).astype(bf16),
                    ],
                    0,
                )
            else:
                p = jnp.exp2(s_edge - best).astype(bf16)
            probs.append(p)
            mixes.append(dot(turned[:, :nk], p).T)
        unscaled = jnp.where(low, mixes[0], mixes[1])
        denom = pltpu.roll(jnp.where(low, mixes[1], mixes[0]), HEAD_DIM, 1)
        inv = 1.0 / denom
        out = unscaled * inv
        mixed_ref[q_span, :] = out.astype(bf16)
        grad = (do_s[q_span, :] * inv).astype(bf16)
        grad_f = grad.astype(f32)
        prod = grad_f * out
        da = jnp.sum(jnp.where(low, prod, 0.0), 1, keepdims=True)
        db = jnp.sum(jnp.where(low, 0.0, prod), 1, keepdims=True)
        da_hi = da.astype(bf16).astype(f32)
        db_hi = db.astype(bf16).astype(f32)
        ga = jnp.where(low, grad_f, 0.0)
        gb = jnp.where(low, 0.0, grad_f)
        ga1 = jnp.where(
            lane == HEAD_DIM, -da_hi, jnp.where(lane == HEAD_DIM + 1, da_hi - da, ga)
        ).astype(bf16)
        gb1 = jnp.where(lane == 0, -db_hi, jnp.where(lane == 1, db_hi - db, gb)).astype(bf16)
        ga = ga.astype(bf16)
        gb = gb.astype(bf16)
        grad_scores = []
        for p, values, g1 in zip(probs, (v_a, v_b), (ga1, gb1)):
            dp = dot(values[:nk, :], g1, NT)
            grad_scores.append((p.astype(f32) * dp).astype(bf16))
        dq = dot(kt_a[:, :nk], grad_scores[0]) + dot(kt_b[:, :nk], grad_scores[1])
        dproj_ref[q_span, :128] = rope(dq.T * score_scale, q_span, True).astype(bf16)
        dk = dot(jnp.concatenate(grad_scores, 1), jnp.concatenate([qa, qb], 0))
        dv = dot(jnp.concatenate(probs, 1), jnp.concatenate([ga, gb], 0))
        if first:
            dk_s[:nk, :] = dk
            dv_s[:nk, :] = dv
        else:
            dk_s[:nk, :] += dk
            dv_s[:nk, :] += dv

    group_keys = seq_len // groups
    per_group = group_keys // rows
    for g in reversed(range(groups)):
        nk = (g + 1) * group_keys
        if g == groups - 1 and per_group > 1:
            dk_s[...] = jnp.zeros_like(dk_s)
            dv_s[...] = jnp.zeros_like(dv_s)
        first = g == groups - 1 and per_group == 1
        if per_group == 1:
            attend(g * group_keys, nk, group_keys, first)
        else:

            def step(j, carry, g=g, nk=nk):
                q0 = pl.multiple_of(g * group_keys + j * rows, rows)
                attend(q0, nk, group_keys, False)
                return carry

            lax.fori_loop(0, per_group, step, 0)

    def finish(j, carry):
        span = pl.ds(pl.multiple_of(j * rows, rows), rows)
        dproj_ref[span, 128:256] = rope(dk_s[span, :] * (1.0 / log2_e), span, True).astype(bf16)
        dproj_ref[span, 256:] = dv_s[span, :].astype(bf16)
        return carry

    lax.fori_loop(0, seq_len // rows, finish, 0)


def attention(scalars, attn_in, cot, pieces, bias, cos, sin, lanes):
    seq_len = attn_in.shape[0]
    fsdp = len(pieces)
    width = bias.shape[1]
    pairs = width // 384
    rows = 256
    groups = 6
    whole = functools.partial(pl.BlockSpec, pipeline_mode=pl.Buffered(1))
    small = pltpu.VMEM((seq_len, 128), bf16)
    turned = pltpu.VMEM((128, seq_len), bf16)
    wide = pltpu.VMEM((seq_len, 128), f32)
    flops = pairs * seq_len * (2 * D * 512 + 12 * 128 * seq_len)
    return pl.pallas_call(
        functools.partial(
            attention_kernel, seq_len=seq_len, rows=rows, groups=groups, fsdp=fsdp, lanes=lanes
        ),
        grid=(pairs,),
        in_specs=[
            pl.BlockSpec(memory_space=pltpu.SMEM),
            whole((seq_len, D), lambda p: (0, 0)),
            whole((seq_len, D), lambda p: (0, 0)),
            pl.BlockSpec((1, 384), lambda p: (0, p)),
            whole((seq_len, 128), lambda p: (0, 0)),
            whole((seq_len, 128), lambda p: (0, 0)),
        ]
        + [pl.BlockSpec(memory_space=pl.ANY)] * fsdp,
        out_specs=[
            pl.BlockSpec((seq_len, 128), lambda p: (0, p)),
            pl.BlockSpec((seq_len, 384), lambda p: (0, p)),
        ],
        out_shape=[
            jax.ShapeDtypeStruct((seq_len, pairs * 128), bf16),
            jax.ShapeDtypeStruct((seq_len, pairs * 384), bf16),
        ],
        scratch_shapes=[
            pltpu.VMEM((D, width), bf16),
            pltpu.VMEM((D + 128, D), bf16),
            pltpu.SemaphoreType.DMA((fsdp, 2)),
        ]
        + [small] * 5 + [turned] * 4 + [wide] * 3,
        compiler_params=pltpu.CompilerParams(vmem_limit_bytes=58 * 1024 * 1024),
        cost_estimate=pl.CostEstimate(
            flops=flops, bytes_accessed=12_000_000, transcendentals=pairs * seq_len * seq_len
        ),
        name="attention",
    )(scalars, attn_in, cot, bias, cos, sin, *pieces)


def mlp_kernel(
    shard_ref,
    rows_ref,
    cot_ref,
    affine_ref,
    bias_ref,
    *refs,
    layout,
    fsdp,
    own_rows,
    unit,
    chunk,
):
    pieces = refs[: len(layout)]
    refs = refs[len(layout) :]
    attn_in_ref, out_ref, grad_in_ref = refs[:3]
    packed_refs = refs[3 : 3 + fsdp]
    mlp_in, mlp_in_t, w_up, w_down, grads_ref, vec_ref, sems, out_sems = refs[3 + fsdp :]
    seq_len = rows_ref.shape[0]
    up_width = fsdp * unit
    folds = unit // own_rows
    rows = 256

    copies = []
    for n, (k, first, count) in enumerate(layout):
        j = shard_ref[0] ^ k
        count = min(count, own_rows - first)
        source = pl.ds(0, count)
        at = pl.ds(pl.multiple_of(j * own_rows + first, 16), count)
        copies.append(
            pltpu.make_async_copy(
                pieces[n].at[source, pl.ds(0, up_width)], w_up.at[at, :], sems.at[n, 0]
            )
        )
        for i in range(folds):
            at = pl.ds(pl.multiple_of(j * unit + i * own_rows + first, 16), count)
            copies.append(
                pltpu.make_async_copy(
                    pieces[n].at[source, pl.ds(up_width + i * D, D)],
                    w_down.at[at, :],
                    sems.at[n, 1 + i],
                )
            )
    for copy in copies:
        copy.start()

    def normed_rows(span):
        x = rows_ref[span, :].astype(f32)
        center = x - jnp.mean(x, -1, keepdims=True)
        return center * lax.rsqrt(jnp.mean(center * center, -1, keepdims=True) + norm_eps)

    def prepare(j, cot_sum):
        span = pl.ds(pl.multiple_of(j * rows, rows), rows)
        normed = normed_rows(span)
        attn_in_ref[span, :] = (normed * affine_ref[0:1, :] + affine_ref[1:2, :]).astype(bf16)
        scaled = normed * affine_ref[2:3, :] + affine_ref[3:4, :]
        mlp_in[span, :] = scaled.astype(bf16)
        mlp_in_t[:, span] = scaled.T.astype(bf16)
        return cot_sum + jnp.sum(cot_ref[span, :].astype(f32), 0, keepdims=True)

    cot_sum = lax.fori_loop(0, seq_len // rows, prepare, jnp.zeros((1, D), f32))
    for copy in copies:
        copy.wait()

    for c in range(up_width // chunk):
        part = slice(c * chunk, (c + 1) * chunk)
        pre_act = dot(mlp_in[...], w_up[:, part]) + bias_ref[:, part]
        cdf = 0.5 + 0.5 * lax.erf(pre_act * inv_sqrt_two)
        hidden = (pre_act * cdf).astype(bf16)
        slope = cdf + pre_act * jnp.exp(-0.5 * pre_act * pre_act) * inv_sqrt_tau
        grad_pre = (dot(cot_ref[...], w_down[part, :], NT) * slope).astype(bf16)
        vec_ref[0:1, part] = jnp.sum(grad_pre.astype(f32), 0, keepdims=True)
        forward = dot(hidden, w_down[part, :])
        backward = dot(grad_pre, w_up[:, part], NT)
        if c == 0:
            out_ref[...] = forward
            grad_in_ref[...] = backward
        else:
            out_ref[...] += forward
            grad_in_ref[...] += backward
        up_grad = dot(mlp_in_t[...], grad_pre).astype(bf16)
        for j in range(fsdp):
            grads_ref[j, :own_rows, part] = up_grad[j * own_rows : (j + 1) * own_rows]
        down_grad = dot(hidden, cot_ref[...], TN).astype(bf16)
        step = math.gcd(own_rows, chunk)
        for r in range(0, chunk, step):
            u = c * chunk + r
            j, i, at = u // unit, u % unit // own_rows, u % own_rows
            grads_ref[j, at : at + step, up_width + i * D : up_width + (i + 1) * D] = down_grad[
                r : r + step
            ]

    def sums(j, carry):
        span = pl.ds(pl.multiple_of(j * rows, rows), rows)
        grad = grad_in_ref[span, :]
        return (
            carry[0] + jnp.sum(grad * normed_rows(span), 0, keepdims=True),
            carry[1] + jnp.sum(grad, 0, keepdims=True),
        )

    none = jnp.zeros((1, D), f32)
    gain_sum, shift_sum = lax.fori_loop(0, seq_len // rows, sums, (none, none))
    row = lax.broadcasted_iota(jnp.int32, (16, D), 0)
    vectors = jnp.where(row == 1, gain_sum, 0.0)
    vectors = jnp.where(row == 2, shift_sum, vectors)
    vectors = jnp.where(row == 3, cot_sum, vectors).astype(bf16)
    row = lax.broadcasted_iota(jnp.int32, (16, unit), 0)
    for j in range(fsdp):
        grads_ref[j, own_rows:, :] = jnp.zeros((16, grads_ref.shape[2]), bf16)
        grads_ref[j, own_rows:, :D] = vectors
        bias = jnp.where(row == 0, vec_ref[0:1, j * unit : (j + 1) * unit], 0.0)
        grads_ref[j, own_rows:, D : D + unit] = bias.astype(bf16)
    copies = [
        pltpu.make_async_copy(
            grads_ref.at[pl.ds(shard_ref[0] ^ k, 1)], packed_refs[k], out_sems.at[k]
        )
        for k in range(fsdp)
    ]
    for copy in copies:
        copy.start()
    for copy in copies:
        copy.wait()


def mlp(shard, rows_in, cot, affine, bias, got, fsdp, unit):
    seq_len = rows_in.shape[0]
    layout = [(k, first, piece.shape[0]) for k, first, piece in got]
    pieces = [piece for _, _, piece in got]
    own_rows = D // fsdp
    packed_width = pieces[0].shape[1]
    up_width = fsdp * unit
    chunk = 256
    vmem = pl.BlockSpec(memory_space=pltpu.VMEM)
    return pl.pallas_call(
        functools.partial(
            mlp_kernel, layout=layout, fsdp=fsdp, own_rows=own_rows, unit=unit, chunk=chunk
        ),
        in_specs=[pl.BlockSpec(memory_space=pltpu.SMEM)]
        + [vmem] * 4
        + [pl.BlockSpec(memory_space=pl.ANY)] * len(pieces),
        out_specs=[vmem] * 3 + [pl.BlockSpec(memory_space=pl.ANY)] * fsdp,
        out_shape=[
            jax.ShapeDtypeStruct((seq_len, D), bf16),
            jax.ShapeDtypeStruct((seq_len, D), f32),
            jax.ShapeDtypeStruct((seq_len, D), f32),
        ]
        + [jax.ShapeDtypeStruct((1, own_rows + 16, packed_width), bf16)] * fsdp,
        scratch_shapes=[
            pltpu.VMEM((seq_len, D), bf16),
            pltpu.VMEM((D, seq_len), bf16),
            pltpu.VMEM((D, up_width), bf16),
            pltpu.VMEM((up_width, D), bf16),
            pltpu.VMEM((fsdp, own_rows + 16, packed_width), bf16),
            pltpu.VMEM((8, up_width), f32),
            pltpu.SemaphoreType.DMA((len(pieces), 1 + unit // own_rows)),
            pltpu.SemaphoreType.DMA((fsdp,)),
        ],
        compiler_params=pltpu.CompilerParams(vmem_limit_bytes=58 * 1024 * 1024),
        cost_estimate=pl.CostEstimate(
            flops=12 * seq_len * D * up_width,
            bytes_accessed=30_000_000,
            transcendentals=2 * seq_len * up_width,
        ),
        name="mlp",
    )(shard, rows_in, cot, affine, bias, *pieces)


def take(x, at, size, axis=0):
    return lax.dynamic_slice_in_dim(x, at * size, size, axis)


def place(out, piece, at, axis=0):
    return lax.dynamic_update_slice_in_dim(out, piece, at * piece.shape[axis], axis)


def swap(x, axis, by):
    n = lax.axis_size(axis)
    return lax.ppermute(x, axis, [(j, j ^ by) for j in range(n)])


def exchange(x, group):
    axis, n, step, me = group
    return [(me ^ s, swap(take(x, me ^ s, 1), axis, s * step) if s else take(x, me, 1)) for s in range(n)]


def gather(x, group):
    axis, n, step, me = group
    return [(me ^ s, swap(x, axis, s * step) if s else x) for s in range(n)]


def gather_rows(x, group):
    axis, n, step, _ = group
    return [(k, 0, swap(x, axis, k * step) if k else x) for k in range(n)]


def stacked(pieces):
    if len(pieces) == 2:
        (me, own), (_, other) = pieces
        first = me == 0
        return jnp.stack([jnp.where(first, own, other), jnp.where(first, other, own)])
    out = jnp.zeros((len(pieces),) + pieces[0][1].shape, pieces[0][1].dtype)
    for j, piece in pieces:
        out = place(out, piece[None], j)
    return out


def after(x, pieces):
    held, arrived = lax.optimization_barrier((x, [piece[-1] for piece in pieces]))
    return held, [piece[:-1] + (got,) for piece, got in zip(pieces, arrived)]


def total(pieces):
    return sum(piece[0].astype(f32) for _, piece in pieces)


def scatter_sum(x, group):
    return total(exchange(x, group))


def rope_tables(seq_len):
    half = ROTARY // 2
    frequency = rope_base ** (-2.0 * np.arange(half) / ROTARY)
    angles = np.arange(seq_len)[:, None] * frequency[None, :]
    cosine, sine = np.cos(angles), np.sin(angles)
    rest = np.zeros((seq_len, HEAD_DIM - ROTARY))
    cos = np.concatenate([cosine, cosine, rest + 1.0] * 2, 1)
    sin = np.concatenate([-sine, sine, rest] * 2, 1)
    return jnp.asarray(cos, f32), jnp.asarray(sin, f32)


def local(
    tokens,
    lengths,
    cotangent,
    qkv_weight,
    qkv_bias,
    out_weight,
    out_bias,
    up_weight,
    up_bias,
    down_weight,
    down_bias,
    attn_gain,
    attn_shift,
    mlp_gain,
    mlp_shift,
):
    seqs, width = tokens.shape[0], tokens.shape[1]
    ctx_size, fsdp = lax.axis_size("ctx"), lax.axis_size("fsdp")
    team = ctx_size // seqs
    here = lax.axis_index("ctx")
    seat, seq = here % team, here // team
    shard = lax.axis_index("fsdp")
    seq_len = ctx_size * width
    heads = HEADS // team
    pairs = (heads + 1) // 2
    lanes = heads * HEAD_DIM
    spare = pairs * 128 - lanes

    def by_pair(x):
        rows = x.shape[0]
        x = take(x.reshape(rows, 3, D), seat, lanes, 2)
        x = jnp.pad(x, ((0, 0), (0, 0), (0, spare)))
        return jnp.concatenate(
            [x[:, t, p * 128 : (p + 1) * 128] for p in range(pairs) for t in range(3)], 1
        )

    unit = FF // (fsdp * team)

    def up_columns(x):
        return jnp.concatenate(
            [take(x[:, j * unit * team : (j + 1) * unit * team], seat, unit, 1) for j in range(fsdp)],
            1,
        )

    seqs_group = ("ctx", seqs, team, seq)
    team_group = ("ctx", team, 1, seat)
    fsdp_group = ("fsdp", fsdp, 1, shard)
    own_rows = D // fsdp
    folds = unit // own_rows

    both = []
    for s in range(seqs):
        block = jnp.concatenate([take(tokens, seq ^ s, 1), take(cotangent, seq ^ s, 1)])
        both.append((seq ^ s, swap(block, "ctx", s * team) if s else block))
    half = stacked(both)
    joined = gather(half, team_group)
    tok_half = half[:, 0]
    rows_in = stacked([(j, h[:, 0]) for j, h in joined]).swapaxes(0, 1).reshape(seq_len, D)
    cot = stacked([(j, h[:, 1]) for j, h in joined]).swapaxes(0, 1).reshape(seq_len, D)

    down_own = take(down_weight, seat, unit)
    mlp_pack = jnp.concatenate(
        [up_columns(up_weight)] + [down_own[i * own_rows : (i + 1) * own_rows] for i in range(folds)],
        1,
    )
    up_width = fsdp * unit
    mlp_width = up_width + folds * D
    vectors = (qkv_bias, out_bias, up_bias, down_bias, attn_gain, attn_shift, mlp_gain, mlp_shift)
    vector_size = sum(v.shape[0] for v in vectors)
    vector_pack = jnp.pad(jnp.concatenate(vectors), (0, mlp_width - vector_size))
    vector_pack = jnp.pad(vector_pack[None], ((0, 31), (0, 0)))
    mlp_pack = jnp.concatenate([mlp_pack, vector_pack], 0)
    mlp_got = gather_rows(mlp_pack, fsdp_group)
    attn_pack = jnp.concatenate([by_pair(qkv_weight), out_weight], 1)
    attn_pack, mlp_got = after(attn_pack, mlp_got)
    attn_got = gather_rows(attn_pack, fsdp_group)
    qkv_width = pairs * 384
    packed = stacked(
        [
            (shard ^ k, piece[own_rows - first, :vector_size])
            for k, first, piece in mlp_got
            if first <= own_rows < first + piece.shape[0]
        ]
    )
    bounds = []
    at = 0
    for v in vectors:
        bounds.append(packed[:, at : at + v.shape[0]].reshape(-1).astype(f32))
        at += v.shape[0]
    full_qkv_b, full_out_b, full_up_b, full_down_b, gain_a, shift_a, gain_m, shift_m = bounds
    b_qkv = by_pair(full_qkv_b[None])
    b_up = up_columns(full_up_b[None])

    def normalise(x):
        x = x.astype(f32)
        center = x - jnp.mean(x, -1, keepdims=True)
        inv = lax.rsqrt(jnp.mean(center * center, -1, keepdims=True) + norm_eps)
        return center * inv, inv

    def columns(x):
        return jnp.sum(x, 0)

    def vector_rows(rows, size):
        out = []
        for at, v in rows:
            v = jnp.broadcast_to(v, (fsdp, v.shape[-1])).astype(bf16)
            out.append(jnp.pad(v, ((0, 0), (at, size - at - v.shape[1])))[:, None])
        return jnp.pad(jnp.concatenate(out, 1), ((0, 0), (0, 16 - len(rows)), (0, 0)))

    normed, _ = normalise(rows_in)
    if seq_len <= 2048:
        affine = jnp.concatenate(
            [gain_a[None], shift_a[None], gain_m[None], shift_m[None], jnp.zeros((4, D), f32)]
        )
        attn_in, mlp_out, grad_mlp_in, *mlp_grads = mlp(
            shard.reshape(1).astype(jnp.int32),
            rows_in,
            cot,
            affine,
            b_up,
            mlp_got,
            fsdp,
            unit,
        )
    else:
        w_up = jnp.zeros((D, up_width), bf16)
        w_down = jnp.zeros((fsdp, folds, own_rows, D), bf16)
        for k, _, piece in mlp_got:
            w_up = place(w_up, piece[:own_rows, :up_width], shard ^ k)
            for i in range(folds):
                part = piece[:own_rows, up_width + i * D : up_width + (i + 1) * D]
                w_down = lax.dynamic_update_slice(w_down, part[None, None], (shard ^ k, i, 0, 0))
        w_down = w_down.reshape(up_width, D)
        attn_in = (normed * gain_a + shift_a).astype(bf16)
        mlp_in = (normed * gain_m + shift_m).astype(bf16)

        pre_act = dot(mlp_in, w_up) + b_up
        cdf = 0.5 * (1.0 + lax.erf(pre_act * inv_sqrt_two))
        hidden = (pre_act * cdf).astype(bf16)
        slope = cdf + pre_act * jnp.exp(-0.5 * pre_act * pre_act) * inv_sqrt_tau
        grad_pre = (dot(cot, w_down, NT) * slope).astype(bf16)
        down_grad = dot(hidden, cot, TN)
        up_grad = dot(mlp_in, grad_pre, TN)
        mlp_out = dot(hidden, w_down)
        grad_mlp_in = dot(grad_pre, w_up, NT)

        mlp_grads = jnp.concatenate(
            [up_grad.astype(bf16).reshape(fsdp, own_rows, up_width)]
            + [
                down_grad.astype(bf16).reshape(fsdp, folds, own_rows, D)[:, i] for i in range(folds)
            ],
            2,
        )
        rows = vector_rows(
            [
                (D, columns(grad_pre.astype(f32)).reshape(fsdp, unit)),
                (0, columns(grad_mlp_in * normed)),
                (0, columns(grad_mlp_in)),
                (0, columns(cot.astype(f32))),
            ],
            mlp_width,
        )
        mlp_grads = jnp.concatenate([mlp_grads, rows], 1)
        mlp_grads = [take(mlp_grads, shard ^ k, 1) for k in range(fsdp)]

    def halve(mine):
        cols = mine.shape[1] // seqs
        block = [take(mine, seq ^ k, cols, 1) for k in range(seqs)]
        got = swap(jnp.stack([block[1], block[3]]), "ctx", team)
        return block[0], block[2], got

    def quarter(own, far, got):
        own = own.astype(f32) + got[0].astype(f32)
        far = far.astype(f32) + got[1].astype(f32)
        return (own + swap(far.astype(bf16), "ctx", 2 * team).astype(f32)).astype(bf16)

    def widen(part):
        return jnp.stack([part, swap(part, "ctx", 2 * team)])

    def whole_again(two):
        got = swap(two, "ctx", team)
        rows, cols = two.shape[1:]
        whole = jnp.zeros((rows, seqs * cols), bf16)
        for k, piece in ((0, two[0]), (2, two[1]), (1, got[0]), (3, got[1])):
            whole = place(whole, piece, seq ^ k, 1)
        return stacked(gather(whole, team_group))

    attn_in, cot_held, mlp_grads, attn_got = lax.optimization_barrier(
        (attn_in, cot, list(mlp_grads), [piece for _, _, piece in attn_got])
    )
    mlp_pieces = [
        (shard ^ k, swap(x, "fsdp", k) if k else x) for k, x in enumerate(mlp_grads)
    ]
    scalars = jnp.stack([lax.dynamic_index_in_dim(lengths, seq, 0, False), shard, seat])
    mixed, grad_proj = attention(
        scalars.astype(jnp.int32), attn_in, cot_held, attn_got, b_qkv, *rope_tables(seq_len), lanes
    )
    (mixed, grad_proj, attn_got), mlp_pieces = after((mixed, grad_proj, attn_got), mlp_pieces)
    mlp_mine = total(mlp_pieces).astype(bf16)
    mixed, grad_proj, mlp_mine = lax.optimization_barrier((mixed, grad_proj, mlp_mine))
    mlp_own, mlp_far, mlp_near = halve(mlp_mine)

    w_qkv = jnp.zeros((D, qkv_width), bf16)
    w_out = jnp.zeros((D, D), bf16)
    for k, piece in enumerate(attn_got):
        w_qkv = place(w_qkv, piece[:, :qkv_width], shard ^ k)
        w_out = place(w_out, piece[:, qkv_width:], shard ^ k)
    w_out_rows = jnp.pad(take(w_out, seat, lanes), ((0, spare), (0, 0)))
    delta_out = mlp_out + dot(mixed, w_out_rows)
    mixed_all = stacked(gather(mixed[:, :lanes], team_group)).swapaxes(0, 1).reshape(seq_len, D)
    grad_proj, mlp_near = lax.optimization_barrier((grad_proj, mlp_near))
    mlp_part = quarter(mlp_own, mlp_far, mlp_near)
    grad_attn_in = dot(grad_proj, w_qkv, NT)
    qkv_grad = dot(attn_in, grad_proj, TN)
    out_cols = D // team
    out_grad = dot(mixed_all, take(cot, seat, out_cols, 1), TN)

    qkv_b_grad = columns(grad_proj.astype(f32))
    qkv_b_grad = jnp.concatenate(
        [
            jnp.concatenate(
                [
                    qkv_b_grad[p * 384 + i * 128 : p * 384 + i * 128 + min(128, lanes - p * 128)]
                    for p in range(pairs)
                ]
            )[None]
            for i in range(3)
        ],
        0,
    )
    qkv_b_grad = place(jnp.zeros((3, D), f32), qkv_b_grad, seat, 1)
    attn_width = qkv_width + out_cols
    attn_grads = jnp.concatenate(
        [
            qkv_grad.astype(bf16).reshape(fsdp, own_rows, qkv_width),
            out_grad.astype(bf16).reshape(fsdp, own_rows, out_cols),
        ],
        2,
    )
    attn_grads = jnp.concatenate(
        [
            attn_grads,
            vector_rows(
                [
                    (0, qkv_b_grad.reshape(fsdp, -1)),
                    (0, columns(grad_attn_in * normed)),
                    (0, columns(grad_attn_in)),
                ],
                attn_width,
            ),
        ],
        1,
    )
    attn_pieces = exchange(attn_grads, fsdp_group)

    def home(x):
        return scatter_sum(x.astype(bf16).reshape(seqs, team, width, D).swapaxes(0, 1), team_group)

    def returned(pieces):
        return stacked([(j, piece[0]) for j, piece in pieces])

    delta_out, mlp_part = lax.optimization_barrier((home(delta_out).astype(bf16), mlp_part))
    out_pieces = exchange(delta_out, seqs_group)

    grad_normed = home(grad_attn_in * gain_a + grad_mlp_in * gain_m)
    normed_half, inv_half = normalise(tok_half)
    delta_in = inv_half * (
        grad_normed
        - jnp.mean(grad_normed, -1, keepdims=True)
        - normed_half * jnp.mean(grad_normed * normed_half, -1, keepdims=True)
    )
    delta_in, out_pieces = after(delta_in.astype(bf16), out_pieces)
    in_pieces = exchange(delta_in, seqs_group)
    layer_out = (
        tokens.astype(f32) + returned(out_pieces).astype(f32) + full_out_b + full_down_b
    ).astype(bf16)

    mlp_all = whole_again(widen(mlp_part))
    attn_mine, in_pieces = after(total(attn_pieces).astype(bf16), in_pieces)
    tokens_grad = cotangent.astype(f32) + returned(in_pieces).astype(f32)
    attn_all = whole_again(widen(quarter(*halve(attn_mine))))

    up_mine = jnp.concatenate(
        [
            mlp_all[t, :own_rows, j * unit : (j + 1) * unit]
            for j in range(fsdp)
            for t in range(team)
        ],
        1,
    ).astype(f32)
    down_mine = jnp.concatenate(
        [
            mlp_all[t, :own_rows, up_width + i * D : up_width + (i + 1) * D]
            for t in range(team)
            for i in range(folds)
        ],
        0,
    ).astype(f32)
    qkv_mine = jnp.concatenate(
        [
            attn_all[
                t, :own_rows, p * 384 + i * 128 : p * 384 + i * 128 + min(128, lanes - p * 128)
            ]
            for i in range(3)
            for t in range(team)
            for p in range(pairs)
        ],
        1,
    ).astype(f32)
    out_mine = jnp.concatenate([attn_all[t, :own_rows, qkv_width:] for t in range(team)], 1).astype(f32)
    mlp_vec = mlp_all[:, own_rows : own_rows + 4].astype(f32)
    up_b_mine = mlp_vec[:, 0, D : D + unit].reshape(-1)
    mlp_vec = take(jnp.sum(mlp_vec[:, 1:, :D], 0), shard, own_rows, 1)
    bias_mine = mlp_vec[2] * (1.0 / team)
    attn_vec = jnp.sum(attn_all[:, own_rows : own_rows + 3].astype(f32), 0)
    qkv_b_mine = attn_vec[0, : 3 * own_rows]
    attn_vec = take(attn_vec[1:, :D], shard, own_rows, 1)

    return (
        layer_out,
        tokens_grad,
        qkv_mine,
        qkv_b_mine,
        out_mine,
        bias_mine,
        up_mine,
        up_b_mine,
        down_mine,
        bias_mine,
        attn_vec[0],
        attn_vec[1],
        mlp_vec[0],
        mlp_vec[1],
    )


def solution(mesh):
    rows, whole = P("fsdp", "ctx", None), P("fsdp", None)
    vector = P("fsdp")
    in_specs = (
        rows,
        vector,
        rows,
        whole,
        vector,
        whole,
        vector,
        whole,
        vector,
        whole,
        vector,
        vector,
        vector,
        vector,
        vector,
    )
    out_specs = (
        rows,
        rows,
        whole,
        vector,
        whole,
        vector,
        whole,
        vector,
        whole,
        vector,
        vector,
        vector,
        vector,
        vector,
    )
    return jax.shard_map(local, mesh=mesh, in_specs=in_specs, out_specs=out_specs, check_vma=False)
```

```python
import functools
import math

import jax
import jax.numpy as jnp
import numpy as np
from jax import lax
from jax.experimental import pallas as pl
from jax.experimental.pallas import tpu as pltpu
from jax.sharding import PartitionSpec as P

D = 768
HEADS = 12
HEAD_DIM = 64
FF = 3072
ROTARY = 16

norm_eps = 1e-05
rope_base = 10000.0
inv_sqrt_two = 0.7071067811865476
inv_sqrt_tau = 0.3989422804014327
log2_e = 1.4426950408889634
masked_bias = -1e30
score_scale = HEAD_DIM ** (-0.5)

f32 = jnp.float32
bf16 = jnp.bfloat16
NT = (((1,), (1,)), ((), ()))
NN = (((1,), (0,)), ((), ()))
TN = (((0,), (0,)), ((), ()))


def dot(a, b, dims=NN):
    return lax.dot_general(a, b, dims, preferred_element_type=f32)


def attention_kernel(
    scalar_ref,
    attn_in_ref,
    cot_ref,
    bias_ref,
    cos_ref,
    sin_ref,
    *refs,
    seq_len,
    rows,
    groups,
    fsdp,
    lanes,
):
    pieces, refs = refs[:fsdp], refs[fsdp:]
    mixed_ref, dproj_ref, w_s, out_w_s, sems = refs[:5]
    scratch = refs[5:]
    q_s, k_a, k_b, v_a, v_b, kt_a, kt_b, vt_a, vt_b, do_s, dk_s, dv_s = scratch
    pair = pl.program_id(0)
    own_rows = D // fsdp
    width = w_s.shape[1]

    @pl.when(pair == 0)
    def _():
        out_w_s[D:, :] = jnp.zeros((128, D), bf16)
        copies = []
        for k in range(fsdp):
            at = pl.ds(pl.multiple_of((scalar_ref[1] ^ k) * own_rows, own_rows), own_rows)
            copies.append(
                pltpu.make_async_copy(
                    pieces[k].at[:, pl.ds(0, width)], w_s.at[at, :], sems.at[k, 0]
                )
            )
            copies.append(
                pltpu.make_async_copy(
                    pieces[k].at[:, pl.ds(width, D)], out_w_s.at[at, :], sems.at[k, 1]
                )
            )
        for copy in copies:
            copy.start()
        for copy in copies:
            copy.wait()

    w_cols = pl.ds(pl.multiple_of(pair * 384, 128), 384)
    out_rows = pl.ds(pl.multiple_of(scalar_ref[2] * lanes + pair * 128, HEAD_DIM), 128)
    live = scalar_ref[0]
    lane = lax.broadcasted_iota(jnp.int32, (rows, 128), 1)
    low = lane < HEAD_DIM
    first_half = lane % HEAD_DIM < ROTARY // 2

    def rope(x, span, back):
        partner = jnp.where(first_half, pltpu.roll(x, 120, 1), pltpu.roll(x, 8, 1))
        partner = partner * sin_ref[span, :]
        turned = x * cos_ref[span, :]
        return turned - partner if back else turned + partner

    def project(j, carry):
        start = pl.multiple_of(j * rows, rows)
        span = pl.ds(start, rows)
        proj = dot(attn_in_ref[span, :], w_s[:, w_cols]) + bias_ref[...]
        q_s[span, :] = (rope(proj[:, :128], span, False) * (score_scale * log2_e)).astype(bf16)
        keys = rope(proj[:, 128:256], span, False)
        values = proj[:, 256:]
        key_pos = start + lax.broadcasted_iota(jnp.int32, (rows, 128), 0)
        dead = jnp.where(key_pos < live, 0.0, masked_bias)
        ka = jnp.where(low, keys, jnp.where(lane == HEAD_DIM, dead, 0.0))
        kb = jnp.where(low, jnp.where(lane == 0, dead, 0.0), keys)
        va = jnp.where(low, values, 1.0)
        vb = jnp.where(low, 1.0, values)
        for src, plain, turned in (
            (ka, k_a, kt_a),
            (kb, k_b, kt_b),
            (va, v_a, vt_a),
            (vb, v_b, vt_b),
        ):
            plain[span, :] = src.astype(bf16)
            turned[:, span] = src.T.astype(bf16)
        do_s[span, :] = dot(cot_ref[span, :], out_w_s[out_rows, :], NT)
        return carry

    lax.fori_loop(0, seq_len // rows, project, 0)

    def attend(q0, nk, group_keys, first):
        q_span = pl.ds(q0, rows)
        queries = q_s[q_span, :].astype(f32)
        zero = jnp.zeros_like(queries)
        qa = jnp.where(low, queries, zero).astype(bf16)
        qb = jnp.where(low, zero, queries).astype(bf16)
        qa1 = jnp.where(low, queries, jnp.where(lane == HEAD_DIM, 1.0, 0.0)).astype(bf16)
        qb1 = jnp.where(low, jnp.where(lane == 0, 1.0, 0.0), queries).astype(bf16)
        edge = nk - group_keys
        key_pos = edge + lax.broadcasted_iota(jnp.int32, (group_keys, rows), 0)
        query_pos = q0 + lax.broadcasted_iota(jnp.int32, (group_keys, rows), 1)
        causal = key_pos <= query_pos
        probs = []
        mixes = []
        for keys, turned, q1 in ((k_a, vt_a, qa1), (k_b, vt_b, qb1)):
            s_edge = dot(keys[edge:nk, :], q1, NT)
            s_edge = jnp.where(causal, s_edge, masked_bias)
            best = jnp.max(s_edge, 0, keepdims=True)
            if edge:
                s_body = dot(keys[:edge, :], q1, NT)
                best = jnp.maximum(best, jnp.max(s_body, 0, keepdims=True))
                p = jnp.concatenate(
                    [
                        jnp.exp2(s_body - best).astype(bf16),
                        jnp.exp2(s_edge - best).astype(bf16),
                    ],
                    0,
                )
            else:
                p = jnp.exp2(s_edge - best).astype(bf16)
            probs.append(p)
            mixes.append(dot(turned[:, :nk], p).T)
        unscaled = jnp.where(low, mixes[0], mixes[1])
        denom = pltpu.roll(jnp.where(low, mixes[1], mixes[0]), HEAD_DIM, 1)
        inv = 1.0 / denom
        out = unscaled * inv
        mixed_ref[q_span, :] = out.astype(bf16)
        grad = (do_s[q_span, :] * inv).astype(bf16)
        grad_f = grad.astype(f32)
        prod = grad_f * out
        da = jnp.sum(jnp.where(low, prod, 0.0), 1, keepdims=True)
        db = jnp.sum(jnp.where(low, 0.0, prod), 1, keepdims=True)
        da_hi = da.astype(bf16).astype(f32)
        db_hi = db.astype(bf16).astype(f32)
        ga = jnp.where(low, grad_f, 0.0)
        gb = jnp.where(low, 0.0, grad_f)
        ga1 = jnp.where(
            lane == HEAD_DIM, -da_hi, jnp.where(lane == HEAD_DIM + 1, da_hi - da, ga)
        ).astype(bf16)
        gb1 = jnp.where(lane == 0, -db_hi, jnp.where(lane == 1, db_hi - db, gb)).astype(bf16)
        ga = ga.astype(bf16)
        gb = gb.astype(bf16)
        grad_scores = []
        for p, values, g1 in zip(probs, (v_a, v_b), (ga1, gb1)):
            dp = dot(values[:nk, :], g1, NT)
            grad_scores.append((p.astype(f32) * dp).astype(bf16))
        dq = dot(kt_a[:, :nk], grad_scores[0]) + dot(kt_b[:, :nk], grad_scores[1])
        dproj_ref[q_span, :128] = rope(dq.T * score_scale, q_span, True).astype(bf16)
        dk = dot(jnp.concatenate(grad_scores, 1), jnp.concatenate([qa, qb], 0))
        dv = dot(jnp.concatenate(probs, 1), jnp.concatenate([ga, gb], 0))
        if first:
            dk_s[:nk, :] = dk
            dv_s[:nk, :] = dv
        else:
            dk_s[:nk, :] += dk
            dv_s[:nk, :] += dv

    group_keys = seq_len // groups
    per_group = group_keys // rows
    for g in reversed(range(groups)):
        nk = (g + 1) * group_keys
        if g == groups - 1 and per_group > 1:
            dk_s[...] = jnp.zeros_like(dk_s)
            dv_s[...] = jnp.zeros_like(dv_s)
        first = g == groups - 1 and per_group == 1
        if per_group == 1:
            attend(g * group_keys, nk, group_keys, first)
        else:

            def step(j, carry, g=g, nk=nk):
                q0 = pl.multiple_of(g * group_keys + j * rows, rows)
                attend(q0, nk, group_keys, False)
                return carry

            lax.fori_loop(0, per_group, step, 0)

    def finish(j, carry):
        span = pl.ds(pl.multiple_of(j * rows, rows), rows)
        dproj_ref[span, 128:256] = rope(dk_s[span, :] * (1.0 / log2_e), span, True).astype(bf16)
        dproj_ref[span, 256:] = dv_s[span, :].astype(bf16)
        return carry

    lax.fori_loop(0, seq_len // rows, finish, 0)


def attention(scalars, attn_in, cot, pieces, bias, cos, sin, lanes):
    seq_len = attn_in.shape[0]
    fsdp = len(pieces)
    width = bias.shape[1]
    pairs = width // 384
    rows = 256
    groups = 6
    whole = functools.partial(pl.BlockSpec, pipeline_mode=pl.Buffered(1))
    small = pltpu.VMEM((seq_len, 128), bf16)
    turned = pltpu.VMEM((128, seq_len), bf16)
    wide = pltpu.VMEM((seq_len, 128), f32)
    flops = pairs * seq_len * (2 * D * 512 + 12 * 128 * seq_len)
    return pl.pallas_call(
        functools.partial(
            attention_kernel, seq_len=seq_len, rows=rows, groups=groups, fsdp=fsdp, lanes=lanes
        ),
        grid=(pairs,),
        in_specs=[
            pl.BlockSpec(memory_space=pltpu.SMEM),
            whole((seq_len, D), lambda p: (0, 0)),
            whole((seq_len, D), lambda p: (0, 0)),
            pl.BlockSpec((1, 384), lambda p: (0, p)),
            whole((seq_len, 128), lambda p: (0, 0)),
            whole((seq_len, 128), lambda p: (0, 0)),
        ]
        + [pl.BlockSpec(memory_space=pl.ANY)] * fsdp,
        out_specs=[
            pl.BlockSpec((seq_len, 128), lambda p: (0, p)),
            pl.BlockSpec((seq_len, 384), lambda p: (0, p)),
        ],
        out_shape=[
            jax.ShapeDtypeStruct((seq_len, pairs * 128), bf16),
            jax.ShapeDtypeStruct((seq_len, pairs * 384), bf16),
        ],
        scratch_shapes=[
            pltpu.VMEM((D, width), bf16),
            pltpu.VMEM((D + 128, D), bf16),
            pltpu.SemaphoreType.DMA((fsdp, 2)),
        ]
        + [small] * 5 + [turned] * 4 + [wide] * 3,
        compiler_params=pltpu.CompilerParams(vmem_limit_bytes=58 * 1024 * 1024),
        cost_estimate=pl.CostEstimate(
            flops=flops, bytes_accessed=12_000_000, transcendentals=pairs * seq_len * seq_len
        ),
        name="attention",
    )(scalars, attn_in, cot, bias, cos, sin, *pieces)


def mlp_kernel(
    shard_ref,
    rows_ref,
    cot_ref,
    affine_ref,
    bias_ref,
    *refs,
    layout,
    fsdp,
    own_rows,
    unit,
    chunk,
):
    pieces = refs[: len(layout)]
    refs = refs[len(layout) :]
    attn_in_ref, out_ref, grad_in_ref = refs[:3]
    packed_refs = refs[3 : 3 + fsdp]
    mlp_in, mlp_in_t, w_up, w_down, grads_ref, vec_ref, sems, out_sems = refs[3 + fsdp :]
    seq_len = rows_ref.shape[0]
    up_width = fsdp * unit
    folds = unit // own_rows
    rows = 256

    copies = []
    for n, (k, first, count) in enumerate(layout):
        j = shard_ref[0] ^ k
        count = min(count, own_rows - first)
        source = pl.ds(0, count)
        at = pl.ds(pl.multiple_of(j * own_rows + first, 16), count)
        copies.append(
            pltpu.make_async_copy(
                pieces[n].at[source, pl.ds(0, up_width)], w_up.at[at, :], sems.at[n, 0]
            )
        )
        for i in range(folds):
            at = pl.ds(pl.multiple_of(j * unit + i * own_rows + first, 16), count)
            copies.append(
                pltpu.make_async_copy(
                    pieces[n].at[source, pl.ds(up_width + i * D, D)],
                    w_down.at[at, :],
                    sems.at[n, 1 + i],
                )
            )
    for copy in copies:
        copy.start()

    def normed_rows(span):
        x = rows_ref[span, :].astype(f32)
        center = x - jnp.mean(x, -1, keepdims=True)
        return center * lax.rsqrt(jnp.mean(center * center, -1, keepdims=True) + norm_eps)

    def prepare(j, cot_sum):
        span = pl.ds(pl.multiple_of(j * rows, rows), rows)
        normed = normed_rows(span)
        attn_in_ref[span, :] = (normed * affine_ref[0:1, :] + affine_ref[1:2, :]).astype(bf16)
        scaled = normed * affine_ref[2:3, :] + affine_ref[3:4, :]
        mlp_in[span, :] = scaled.astype(bf16)
        mlp_in_t[:, span] = scaled.T.astype(bf16)
        return cot_sum + jnp.sum(cot_ref[span, :].astype(f32), 0, keepdims=True)

    cot_sum = lax.fori_loop(0, seq_len // rows, prepare, jnp.zeros((1, D), f32))
    for copy in copies:
        copy.wait()

    for c in range(up_width // chunk):
        part = slice(c * chunk, (c + 1) * chunk)
        pre_act = dot(mlp_in[...], w_up[:, part]) + bias_ref[:, part]
        cdf = 0.5 + 0.5 * lax.erf(pre_act * inv_sqrt_two)
        hidden = (pre_act * cdf).astype(bf16)
        slope = cdf + pre_act * jnp.exp(-0.5 * pre_act * pre_act) * inv_sqrt_tau
        grad_pre = (dot(cot_ref[...], w_down[part, :], NT) * slope).astype(bf16)
        vec_ref[0:1, part] = jnp.sum(grad_pre.astype(f32), 0, keepdims=True)
        forward = dot(hidden, w_down[part, :])
        backward = dot(grad_pre, w_up[:, part], NT)
        if c == 0:
            out_ref[...] = forward
            grad_in_ref[...] = backward
        else:
            out_ref[...] += forward
            grad_in_ref[...] += backward
        up_grad = dot(mlp_in_t[...], grad_pre).astype(bf16)
        for j in range(fsdp):
            grads_ref[j, :own_rows, part] = up_grad[j * own_rows : (j + 1) * own_rows]
        down_grad = dot(hidden, cot_ref[...], TN).astype(bf16)
        step = math.gcd(own_rows, chunk)
        for r in range(0, chunk, step):
            u = c * chunk + r
            j, i, at = u // unit, u % unit // own_rows, u % own_rows
            grads_ref[j, at : at + step, up_width + i * D : up_width + (i + 1) * D] = down_grad[
                r : r + step
            ]

    def sums(j, carry):
        span = pl.ds(pl.multiple_of(j * rows, rows), rows)
        grad = grad_in_ref[span, :]
        return (
            carry[0] + jnp.sum(grad * normed_rows(span), 0, keepdims=True),
            carry[1] + jnp.sum(grad, 0, keepdims=True),
        )

    none = jnp.zeros((1, D), f32)
    gain_sum, shift_sum = lax.fori_loop(0, seq_len // rows, sums, (none, none))
    row = lax.broadcasted_iota(jnp.int32, (16, D), 0)
    vectors = jnp.where(row == 1, gain_sum, 0.0)
    vectors = jnp.where(row == 2, shift_sum, vectors)
    vectors = jnp.where(row == 3, cot_sum, vectors).astype(bf16)
    row = lax.broadcasted_iota(jnp.int32, (16, unit), 0)
    for j in range(fsdp):
        grads_ref[j, own_rows:, :] = jnp.zeros((16, grads_ref.shape[2]), bf16)
        grads_ref[j, own_rows:, :D] = vectors
        bias = jnp.where(row == 0, vec_ref[0:1, j * unit : (j + 1) * unit], 0.0)
        grads_ref[j, own_rows:, D : D + unit] = bias.astype(bf16)
    copies = [
        pltpu.make_async_copy(
            grads_ref.at[pl.ds(shard_ref[0] ^ k, 1)], packed_refs[k], out_sems.at[k]
        )
        for k in range(fsdp)
    ]
    for copy in copies:
        copy.start()
    for copy in copies:
        copy.wait()


def mlp(shard, rows_in, cot, affine, bias, got, fsdp, unit):
    seq_len = rows_in.shape[0]
    layout = [(k, first, piece.shape[0]) for k, first, piece in got]
    pieces = [piece for _, _, piece in got]
    own_rows = D // fsdp
    packed_width = pieces[0].shape[1]
    up_width = fsdp * unit
    chunk = 256
    vmem = pl.BlockSpec(memory_space=pltpu.VMEM)
    return pl.pallas_call(
        functools.partial(
            mlp_kernel, layout=layout, fsdp=fsdp, own_rows=own_rows, unit=unit, chunk=chunk
        ),
        in_specs=[pl.BlockSpec(memory_space=pltpu.SMEM)]
        + [vmem] * 4
        + [pl.BlockSpec(memory_space=pl.ANY)] * len(pieces),
        out_specs=[vmem] * 3 + [pl.BlockSpec(memory_space=pl.ANY)] * fsdp,
        out_shape=[
            jax.ShapeDtypeStruct((seq_len, D), bf16),
            jax.ShapeDtypeStruct((seq_len, D), f32),
            jax.ShapeDtypeStruct((seq_len, D), f32),
        ]
        + [jax.ShapeDtypeStruct((1, own_rows + 16, packed_width), bf16)] * fsdp,
        scratch_shapes=[
            pltpu.VMEM((seq_len, D), bf16),
            pltpu.VMEM((D, seq_len), bf16),
            pltpu.VMEM((D, up_width), bf16),
            pltpu.VMEM((up_width, D), bf16),
            pltpu.VMEM((fsdp, own_rows + 16, packed_width), bf16),
            pltpu.VMEM((8, up_width), f32),
            pltpu.SemaphoreType.DMA((len(pieces), 1 + unit // own_rows)),
            pltpu.SemaphoreType.DMA((fsdp,)),
        ],
        compiler_params=pltpu.CompilerParams(vmem_limit_bytes=58 * 1024 * 1024),
        cost_estimate=pl.CostEstimate(
            flops=12 * seq_len * D * up_width,
            bytes_accessed=30_000_000,
            transcendentals=2 * seq_len * up_width,
        ),
        name="mlp",
    )(shard, rows_in, cot, affine, bias, *pieces)


def take(x, at, size, axis=0):
    return lax.dynamic_slice_in_dim(x, at * size, size, axis)


def place(out, piece, at, axis=0):
    return lax.dynamic_update_slice_in_dim(out, piece, at * piece.shape[axis], axis)


def swap(x, axis, by):
    n = lax.axis_size(axis)
    return lax.ppermute(x, axis, [(j, j ^ by) for j in range(n)])


def exchange(x, group):
    axis, n, step, me = group
    return [(me ^ s, swap(take(x, me ^ s, 1), axis, s * step) if s else take(x, me, 1)) for s in range(n)]


def gather(x, group):
    axis, n, step, me = group
    return [(me ^ s, swap(x, axis, s * step) if s else x) for s in range(n)]


def gather_rows(x, group):
    axis, n, step, _ = group
    return [(k, 0, swap(x, axis, k * step) if k else x) for k in range(n)]


def stacked(pieces):
    if len(pieces) == 2:
        (me, own), (_, other) = pieces
        first = me == 0
        return jnp.stack([jnp.where(first, own, other), jnp.where(first, other, own)])
    out = jnp.zeros((len(pieces),) + pieces[0][1].shape, pieces[0][1].dtype)
    for j, piece in pieces:
        out = place(out, piece[None], j)
    return out


def after(x, pieces):
    held, arrived = lax.optimization_barrier((x, [piece[-1] for piece in pieces]))
    return held, [piece[:-1] + (got,) for piece, got in zip(pieces, arrived)]


def total(pieces):
    return sum(piece[0].astype(f32) for _, piece in pieces)


def scatter_sum(x, group):
    return total(exchange(x, group))


def rope_tables(seq_len):
    half = ROTARY // 2
    frequency = rope_base ** (-2.0 * np.arange(half) / ROTARY)
    angles = np.arange(seq_len)[:, None] * frequency[None, :]
    cosine, sine = np.cos(angles), np.sin(angles)
    rest = np.zeros((seq_len, HEAD_DIM - ROTARY))
    cos = np.concatenate([cosine, cosine, rest + 1.0] * 2, 1)
    sin = np.concatenate([-sine, sine, rest] * 2, 1)
    return jnp.asarray(cos, f32), jnp.asarray(sin, f32)


def local(
    tokens,
    lengths,
    cotangent,
    qkv_weight,
    qkv_bias,
    out_weight,
    out_bias,
    up_weight,
    up_bias,
    down_weight,
    down_bias,
    attn_gain,
    attn_shift,
    mlp_gain,
    mlp_shift,
):
    seqs, width = tokens.shape[0], tokens.shape[1]
    ctx_size, fsdp = lax.axis_size("ctx"), lax.axis_size("fsdp")
    team = ctx_size // seqs
    here = lax.axis_index("ctx")
    seat, seq = here % team, here // team
    shard = lax.axis_index("fsdp")
    seq_len = ctx_size * width
    heads = HEADS // team
    pairs = (heads + 1) // 2
    lanes = heads * HEAD_DIM
    spare = pairs * 128 - lanes

    def by_pair(x):
        rows = x.shape[0]
        x = take(x.reshape(rows, 3, D), seat, lanes, 2)
        x = jnp.pad(x, ((0, 0), (0, 0), (0, spare)))
        return jnp.concatenate(
            [x[:, t, p * 128 : (p + 1) * 128] for p in range(pairs) for t in range(3)], 1
        )

    unit = FF // (fsdp * team)

    def up_columns(x):
        return jnp.concatenate(
            [take(x[:, j * unit * team : (j + 1) * unit * team], seat, unit, 1) for j in range(fsdp)],
            1,
        )

    seqs_group = ("ctx", seqs, team, seq)
    team_group = ("ctx", team, 1, seat)
    fsdp_group = ("fsdp", fsdp, 1, shard)
    own_rows = D // fsdp
    folds = unit // own_rows

    blocks = [
        jnp.concatenate([take(tokens, seq ^ s, 1), take(cotangent, seq ^ s, 1)]) for s in range(seqs)
    ]
    both = [(seq ^ s, swap(x, "ctx", s * team) if s else x) for s, x in enumerate(blocks)]
    blocks, up_weight, down_weight = lax.optimization_barrier((blocks, up_weight, down_weight))
    half = stacked(both)
    joined = gather(half, team_group)
    tok_half = half[:, 0]
    rows_in = stacked([(j, h[:, 0]) for j, h in joined]).swapaxes(0, 1).reshape(seq_len, D)
    cot = stacked([(j, h[:, 1]) for j, h in joined]).swapaxes(0, 1).reshape(seq_len, D)

    down_own = take(down_weight, seat, unit)
    mlp_pack = jnp.concatenate(
        [up_columns(up_weight)] + [down_own[i * own_rows : (i + 1) * own_rows] for i in range(folds)],
        1,
    )
    up_width = fsdp * unit
    mlp_width = up_width + folds * D
    vectors = (qkv_bias, out_bias, up_bias, down_bias, attn_gain, attn_shift, mlp_gain, mlp_shift)
    vector_size = sum(v.shape[0] for v in vectors)
    vector_pack = jnp.pad(jnp.concatenate(vectors), (0, mlp_width - vector_size))
    vector_pack = jnp.pad(vector_pack[None], ((0, 31), (0, 0)))
    mlp_pack = jnp.concatenate([mlp_pack, vector_pack], 0)
    mlp_got = gather_rows(mlp_pack, fsdp_group)
    attn_pack = jnp.concatenate([by_pair(qkv_weight), out_weight], 1)
    attn_pack, mlp_got = after(attn_pack, mlp_got)
    attn_got = gather_rows(attn_pack, fsdp_group)
    qkv_width = pairs * 384
    packed = stacked(
        [
            (shard ^ k, piece[own_rows - first, :vector_size])
            for k, first, piece in mlp_got
            if first <= own_rows < first + piece.shape[0]
        ]
    )
    bounds = []
    at = 0
    for v in vectors:
        bounds.append(packed[:, at : at + v.shape[0]].reshape(-1).astype(f32))
        at += v.shape[0]
    full_qkv_b, full_out_b, full_up_b, full_down_b, gain_a, shift_a, gain_m, shift_m = bounds
    b_qkv = by_pair(full_qkv_b[None])
    b_up = up_columns(full_up_b[None])

    def normalise(x):
        x = x.astype(f32)
        center = x - jnp.mean(x, -1, keepdims=True)
        inv = lax.rsqrt(jnp.mean(center * center, -1, keepdims=True) + norm_eps)
        return center * inv, inv

    def columns(x):
        return jnp.sum(x, 0)

    def vector_rows(rows, size):
        out = []
        for at, v in rows:
            v = jnp.broadcast_to(v, (fsdp, v.shape[-1])).astype(bf16)
            out.append(jnp.pad(v, ((0, 0), (at, size - at - v.shape[1])))[:, None])
        return jnp.pad(jnp.concatenate(out, 1), ((0, 0), (0, 16 - len(rows)), (0, 0)))

    normed, _ = normalise(rows_in)
    if seq_len <= 2048:
        affine = jnp.concatenate(
            [gain_a[None], shift_a[None], gain_m[None], shift_m[None], jnp.zeros((4, D), f32)]
        )
        attn_in, mlp_out, grad_mlp_in, *mlp_grads = mlp(
            shard.reshape(1).astype(jnp.int32),
            rows_in,
            cot,
            affine,
            b_up,
            mlp_got,
            fsdp,
            unit,
        )
    else:
        w_up = jnp.zeros((D, up_width), bf16)
        w_down = jnp.zeros((fsdp, folds, own_rows, D), bf16)
        for k, _, piece in mlp_got:
            w_up = place(w_up, piece[:own_rows, :up_width], shard ^ k)
            for i in range(folds):
                part = piece[:own_rows, up_width + i * D : up_width + (i + 1) * D]
                w_down = lax.dynamic_update_slice(w_down, part[None, None], (shard ^ k, i, 0, 0))
        w_down = w_down.reshape(up_width, D)
        attn_in = (normed * gain_a + shift_a).astype(bf16)
        mlp_in = (normed * gain_m + shift_m).astype(bf16)

        pre_act = dot(mlp_in, w_up) + b_up
        cdf = 0.5 * (1.0 + lax.erf(pre_act * inv_sqrt_two))
        hidden = (pre_act * cdf).astype(bf16)
        slope = cdf + pre_act * jnp.exp(-0.5 * pre_act * pre_act) * inv_sqrt_tau
        grad_pre = (dot(cot, w_down, NT) * slope).astype(bf16)
        down_grad = dot(hidden, cot, TN)
        up_grad = dot(mlp_in, grad_pre, TN)
        mlp_out = dot(hidden, w_down)
        grad_mlp_in = dot(grad_pre, w_up, NT)

        mlp_grads = jnp.concatenate(
            [up_grad.astype(bf16).reshape(fsdp, own_rows, up_width)]
            + [
                down_grad.astype(bf16).reshape(fsdp, folds, own_rows, D)[:, i] for i in range(folds)
            ],
            2,
        )
        rows = vector_rows(
            [
                (D, columns(grad_pre.astype(f32)).reshape(fsdp, unit)),
                (0, columns(grad_mlp_in * normed)),
                (0, columns(grad_mlp_in)),
                (0, columns(cot.astype(f32))),
            ],
            mlp_width,
        )
        mlp_grads = jnp.concatenate([mlp_grads, rows], 1)
        mlp_grads = [take(mlp_grads, shard ^ k, 1) for k in range(fsdp)]

    def halve(mine):
        cols = mine.shape[1] // seqs
        block = [take(mine, seq ^ k, cols, 1) for k in range(seqs)]
        got = swap(jnp.stack([block[1], block[3]]), "ctx", team)
        return block[0], block[2], got

    def quarter(own, far, got):
        own = own.astype(f32) + got[0].astype(f32)
        far = far.astype(f32) + got[1].astype(f32)
        return (own + swap(far.astype(bf16), "ctx", 2 * team).astype(f32)).astype(bf16)

    def widen(part):
        return jnp.stack([part, swap(part, "ctx", 2 * team)])

    def whole_again(two):
        got = swap(two, "ctx", team)
        rows, cols = two.shape[1:]
        whole = jnp.zeros((rows, seqs * cols), bf16)
        for k, piece in ((0, two[0]), (2, two[1]), (1, got[0]), (3, got[1])):
            whole = place(whole, piece, seq ^ k, 1)
        return stacked(gather(whole, team_group))

    attn_in, cot_held, mlp_grads, attn_got = lax.optimization_barrier(
        (attn_in, cot, list(mlp_grads), [piece for _, _, piece in attn_got])
    )
    mlp_pieces = [
        (shard ^ k, swap(x, "fsdp", k) if k else x) for k, x in enumerate(mlp_grads)
    ]
    scalars = jnp.stack([lax.dynamic_index_in_dim(lengths, seq, 0, False), shard, seat])
    mixed, grad_proj = attention(
        scalars.astype(jnp.int32), attn_in, cot_held, attn_got, b_qkv, *rope_tables(seq_len), lanes
    )
    (mixed, grad_proj, attn_got), mlp_pieces = after((mixed, grad_proj, attn_got), mlp_pieces)
    mlp_mine = total(mlp_pieces).astype(bf16)
    mixed, grad_proj, mlp_mine = lax.optimization_barrier((mixed, grad_proj, mlp_mine))
    mlp_own, mlp_far, mlp_near = halve(mlp_mine)

    w_qkv = jnp.zeros((D, qkv_width), bf16)
    w_out = jnp.zeros((D, D), bf16)
    for k, piece in enumerate(attn_got):
        w_qkv = place(w_qkv, piece[:, :qkv_width], shard ^ k)
        w_out = place(w_out, piece[:, qkv_width:], shard ^ k)
    w_out_rows = jnp.pad(take(w_out, seat, lanes), ((0, spare), (0, 0)))
    delta_out = mlp_out + dot(mixed, w_out_rows)
    mixed_got = gather(mixed[:, :lanes], team_group)
    grad_proj, mlp_near = lax.optimization_barrier((grad_proj, mlp_near))
    mlp_part = quarter(mlp_own, mlp_far, mlp_near)
    grad_attn_in = dot(grad_proj, w_qkv, NT)
    qkv_grad = dot(attn_in, grad_proj, TN)
    out_cols = D // team
    cot_cols = take(cot, seat, out_cols, 1)
    out_grad = stacked([(j, dot(m, cot_cols, TN).astype(bf16)) for j, m in mixed_got])

    qkv_b_grad = columns(grad_proj.astype(f32))
    qkv_b_grad = jnp.concatenate(
        [
            jnp.concatenate(
                [
                    qkv_b_grad[p * 384 + i * 128 : p * 384 + i * 128 + min(128, lanes - p * 128)]
                    for p in range(pairs)
                ]
            )[None]
            for i in range(3)
        ],
        0,
    )
    qkv_b_grad = place(jnp.zeros((3, D), f32), qkv_b_grad, seat, 1)
    attn_width = qkv_width + out_cols
    attn_grads = jnp.concatenate(
        [
            qkv_grad.astype(bf16).reshape(fsdp, own_rows, qkv_width),
            out_grad.astype(bf16).reshape(fsdp, own_rows, out_cols),
        ],
        2,
    )
    attn_grads = jnp.concatenate(
        [
            attn_grads,
            vector_rows(
                [
                    (0, qkv_b_grad.reshape(fsdp, -1)),
                    (0, columns(grad_attn_in * normed)),
                    (0, columns(grad_attn_in)),
                ],
                attn_width,
            ),
        ],
        1,
    )
    attn_pieces = exchange(attn_grads, fsdp_group)

    def home(x):
        return scatter_sum(x.astype(bf16).reshape(seqs, team, width, D).swapaxes(0, 1), team_group)

    def returned(pieces):
        return stacked([(j, piece[0]) for j, piece in pieces])

    delta_out, mlp_part = lax.optimization_barrier((home(delta_out).astype(bf16), mlp_part))
    out_pieces = exchange(delta_out, seqs_group)

    grad_normed = home(grad_attn_in * gain_a + grad_mlp_in * gain_m)
    normed_half, inv_half = normalise(tok_half)
    delta_in = inv_half * (
        grad_normed
        - jnp.mean(grad_normed, -1, keepdims=True)
        - normed_half * jnp.mean(grad_normed * normed_half, -1, keepdims=True)
    )
    delta_in, out_pieces = after(delta_in.astype(bf16), out_pieces)
    in_pieces = exchange(delta_in, seqs_group)
    layer_out = (
        tokens.astype(f32) + returned(out_pieces).astype(f32) + full_out_b + full_down_b
    ).astype(bf16)

    mlp_two, attn_pieces = after(widen(mlp_part), attn_pieces)
    attn_mine = total(attn_pieces).astype(bf16)
    attn_own, attn_far, attn_near = halve(attn_mine)
    mlp_all = whole_again(mlp_two)
    tokens_grad = cotangent.astype(f32) + returned(in_pieces).astype(f32)
    attn_all = whole_again(widen(quarter(attn_own, attn_far, attn_near)))

    up_mine = jnp.concatenate(
        [
            mlp_all[t, :own_rows, j * unit : (j + 1) * unit]
            for j in range(fsdp)
            for t in range(team)
        ],
        1,
    ).astype(f32)
    down_mine = jnp.concatenate(
        [
            mlp_all[t, :own_rows, up_width + i * D : up_width + (i + 1) * D]
            for t in range(team)
            for i in range(folds)
        ],
        0,
    ).astype(f32)
    qkv_mine = jnp.concatenate(
        [
            attn_all[
                t, :own_rows, p * 384 + i * 128 : p * 384 + i * 128 + min(128, lanes - p * 128)
            ]
            for i in range(3)
            for t in range(team)
            for p in range(pairs)
        ],
        1,
    ).astype(f32)
    out_mine = jnp.concatenate([attn_all[t, :own_rows, qkv_width:] for t in range(team)], 1).astype(f32)
    mlp_vec = mlp_all[:, own_rows : own_rows + 4].astype(f32)
    up_b_mine = mlp_vec[:, 0, D : D + unit].reshape(-1)
    mlp_vec = take(jnp.sum(mlp_vec[:, 1:, :D], 0), shard, own_rows, 1)
    bias_mine = mlp_vec[2] * (1.0 / team)
    attn_vec = jnp.sum(attn_all[:, own_rows : own_rows + 3].astype(f32), 0)
    qkv_b_mine = attn_vec[0, : 3 * own_rows]
    attn_vec = take(attn_vec[1:, :D], shard, own_rows, 1)

    return (
        layer_out,
        tokens_grad,
        qkv_mine,
        qkv_b_mine,
        out_mine,
        bias_mine,
        up_mine,
        up_b_mine,
        down_mine,
        bias_mine,
        attn_vec[0],
        attn_vec[1],
        mlp_vec[0],
        mlp_vec[1],
    )


def solution(mesh):
    rows, whole = P("fsdp", "ctx", None), P("fsdp", None)
    vector = P("fsdp")
    in_specs = (
        rows,
        vector,
        rows,
        whole,
        vector,
        whole,
        vector,
        whole,
        vector,
        whole,
        vector,
        vector,
        vector,
        vector,
        vector,
    )
    out_specs = (
        rows,
        rows,
        whole,
        vector,
        whole,
        vector,
        whole,
        vector,
        whole,
        vector,
        vector,
        vector,
        vector,
        vector,
    )
    return jax.shard_map(local, mesh=mesh, in_specs=in_specs, out_specs=out_specs, check_vma=False)
```

```python
import functools
import math

import jax
import jax.numpy as jnp
import numpy as np
from jax import lax
from jax.experimental import pallas as pl
from jax.experimental.pallas import tpu as pltpu
from jax.sharding import PartitionSpec as P

D = 768
HEADS = 12
HEAD_DIM = 64
FF = 3072
ROTARY = 16

norm_eps = 1e-05
rope_base = 10000.0
inv_sqrt_two = 0.7071067811865476
inv_sqrt_tau = 0.3989422804014327
log2_e = 1.4426950408889634
masked_bias = -1e30
score_scale = HEAD_DIM ** (-0.5)

f32 = jnp.float32
bf16 = jnp.bfloat16
NT = (((1,), (1,)), ((), ()))
NN = (((1,), (0,)), ((), ()))
TN = (((0,), (0,)), ((), ()))


def dot(a, b, dims=NN):
    return lax.dot_general(a, b, dims, preferred_element_type=f32)


def attention_kernel(
    scalar_ref,
    attn_in_ref,
    cot_ref,
    bias_ref,
    cos_ref,
    sin_ref,
    *refs,
    seq_len,
    rows,
    groups,
    fsdp,
    lanes,
):
    pieces, refs = refs[:fsdp], refs[fsdp:]
    mixed_ref, dproj_ref, w_s, out_w_s, sems = refs[:5]
    scratch = refs[5:]
    q_s, k_a, k_b, v_a, v_b, kt_a, kt_b, vt_a, vt_b, do_s, dk_s, dv_s = scratch
    pair = pl.program_id(0)
    own_rows = D // fsdp
    width = w_s.shape[1]

    @pl.when(pair == 0)
    def _():
        out_w_s[D:, :] = jnp.zeros((128, D), bf16)
        copies = []
        for k in range(fsdp):
            at = pl.ds(pl.multiple_of((scalar_ref[1] ^ k) * own_rows, own_rows), own_rows)
            copies.append(
                pltpu.make_async_copy(
                    pieces[k].at[:, pl.ds(0, width)], w_s.at[at, :], sems.at[k, 0]
                )
            )
            copies.append(
                pltpu.make_async_copy(
                    pieces[k].at[:, pl.ds(width, D)], out_w_s.at[at, :], sems.at[k, 1]
                )
            )
        for copy in copies:
            copy.start()
        for copy in copies:
            copy.wait()

    w_cols = pl.ds(pl.multiple_of(pair * 384, 128), 384)
    out_rows = pl.ds(pl.multiple_of(scalar_ref[2] * lanes + pair * 128, HEAD_DIM), 128)
    live = scalar_ref[0]
    lane = lax.broadcasted_iota(jnp.int32, (rows, 128), 1)
    low = lane < HEAD_DIM
    first_half = lane % HEAD_DIM < ROTARY // 2

    def rope(x, span, back):
        partner = jnp.where(first_half, pltpu.roll(x, 120, 1), pltpu.roll(x, 8, 1))
        partner = partner * sin_ref[span, :]
        turned = x * cos_ref[span, :]
        return turned - partner if back else turned + partner

    def project(j, carry):
        start = pl.multiple_of(j * rows, rows)
        span = pl.ds(start, rows)
        proj = dot(attn_in_ref[span, :], w_s[:, w_cols]) + bias_ref[...]
        q_s[span, :] = (rope(proj[:, :128], span, False) * (score_scale * log2_e)).astype(bf16)
        keys = rope(proj[:, 128:256], span, False)
        values = proj[:, 256:]
        key_pos = start + lax.broadcasted_iota(jnp.int32, (rows, 128), 0)
        dead = jnp.where(key_pos < live, 0.0, masked_bias)
        ka = jnp.where(low, keys, jnp.where(lane == HEAD_DIM, dead, 0.0))
        kb = jnp.where(low, jnp.where(lane == 0, dead, 0.0), keys)
        va = jnp.where(low, values, 1.0)
        vb = jnp.where(low, 1.0, values)
        for src, plain, turned in (
            (ka, k_a, kt_a),
            (kb, k_b, kt_b),
            (va, v_a, vt_a),
            (vb, v_b, vt_b),
        ):
            plain[span, :] = src.astype(bf16)
            turned[:, span] = src.T.astype(bf16)
        do_s[span, :] = dot(cot_ref[span, :], out_w_s[out_rows, :], NT)
        return carry

    lax.fori_loop(0, seq_len // rows, project, 0)

    def attend(q0, nk, group_keys, first):
        q_span = pl.ds(q0, rows)
        queries = q_s[q_span, :].astype(f32)
        zero = jnp.zeros_like(queries)
        qa = jnp.where(low, queries, zero).astype(bf16)
        qb = jnp.where(low, zero, queries).astype(bf16)
        qa1 = jnp.where(low, queries, jnp.where(lane == HEAD_DIM, 1.0, 0.0)).astype(bf16)
        qb1 = jnp.where(low, jnp.where(lane == 0, 1.0, 0.0), queries).astype(bf16)
        edge = nk - group_keys
        key_pos = edge + lax.broadcasted_iota(jnp.int32, (group_keys, rows), 0)
        query_pos = q0 + lax.broadcasted_iota(jnp.int32, (group_keys, rows), 1)
        causal = key_pos <= query_pos
        probs = []
        mixes = []
        for keys, turned, q1 in ((k_a, vt_a, qa1), (k_b, vt_b, qb1)):
            s_edge = dot(keys[edge:nk, :], q1, NT)
            s_edge = jnp.where(causal, s_edge, masked_bias)
            best = jnp.max(s_edge, 0, keepdims=True)
            if edge:
                s_body = dot(keys[:edge, :], q1, NT)
                best = jnp.maximum(best, jnp.max(s_body, 0, keepdims=True))
                p = jnp.concatenate(
                    [
                        jnp.exp2(s_body - best).astype(bf16),
                        jnp.exp2(s_edge - best).astype(bf16),
                    ],
                    0,
                )
            else:
                p = jnp.exp2(s_edge - best).astype(bf16)
            probs.append(p)
            mixes.append(dot(turned[:, :nk], p).T)
        unscaled = jnp.where(low, mixes[0], mixes[1])
        denom = pltpu.roll(jnp.where(low, mixes[1], mixes[0]), HEAD_DIM, 1)
        inv = 1.0 / denom
        out = unscaled * inv
        mixed_ref[q_span, :] = out.astype(bf16)
        grad = (do_s[q_span, :] * inv).astype(bf16)
        grad_f = grad.astype(f32)
        prod = grad_f * out
        da = jnp.sum(jnp.where(low, prod, 0.0), 1, keepdims=True)
        db = jnp.sum(jnp.where(low, 0.0, prod), 1, keepdims=True)
        da_hi = da.astype(bf16).astype(f32)
        db_hi = db.astype(bf16).astype(f32)
        ga = jnp.where(low, grad_f, 0.0)
        gb = jnp.where(low, 0.0, grad_f)
        ga1 = jnp.where(
            lane == HEAD_DIM, -da_hi, jnp.where(lane == HEAD_DIM + 1, da_hi - da, ga)
        ).astype(bf16)
        gb1 = jnp.where(lane == 0, -db_hi, jnp.where(lane == 1, db_hi - db, gb)).astype(bf16)
        ga = ga.astype(bf16)
        gb = gb.astype(bf16)
        grad_scores = []
        for p, values, g1 in zip(probs, (v_a, v_b), (ga1, gb1)):
            dp = dot(values[:nk, :], g1, NT)
            grad_scores.append((p.astype(f32) * dp).astype(bf16))
        dq = dot(kt_a[:, :nk], grad_scores[0]) + dot(kt_b[:, :nk], grad_scores[1])
        dproj_ref[q_span, :128] = rope(dq.T * score_scale, q_span, True).astype(bf16)
        dk = dot(jnp.concatenate(grad_scores, 1), jnp.concatenate([qa, qb], 0))
        dv = dot(jnp.concatenate(probs, 1), jnp.concatenate([ga, gb], 0))
        if first:
            dk_s[:nk, :] = dk
            dv_s[:nk, :] = dv
        else:
            dk_s[:nk, :] += dk
            dv_s[:nk, :] += dv

    group_keys = seq_len // groups
    per_group = group_keys // rows
    for g in reversed(range(groups)):
        nk = (g + 1) * group_keys
        if g == groups - 1 and per_group > 1:
            dk_s[...] = jnp.zeros_like(dk_s)
            dv_s[...] = jnp.zeros_like(dv_s)
        first = g == groups - 1 and per_group == 1
        if per_group == 1:
            attend(g * group_keys, nk, group_keys, first)
        else:

            def step(j, carry, g=g, nk=nk):
                q0 = pl.multiple_of(g * group_keys + j * rows, rows)
                attend(q0, nk, group_keys, False)
                return carry

            lax.fori_loop(0, per_group, step, 0)

    def finish(j, carry):
        span = pl.ds(pl.multiple_of(j * rows, rows), rows)
        dproj_ref[span, 128:256] = rope(dk_s[span, :] * (1.0 / log2_e), span, True).astype(bf16)
        dproj_ref[span, 256:] = dv_s[span, :].astype(bf16)
        return carry

    lax.fori_loop(0, seq_len // rows, finish, 0)


def attention(scalars, attn_in, cot, pieces, bias, cos, sin, lanes):
    seq_len = attn_in.shape[0]
    fsdp = len(pieces)
    width = bias.shape[1]
    pairs = width // 384
    rows = 256
    groups = 6
    whole = functools.partial(pl.BlockSpec, pipeline_mode=pl.Buffered(1))
    small = pltpu.VMEM((seq_len, 128), bf16)
    turned = pltpu.VMEM((128, seq_len), bf16)
    wide = pltpu.VMEM((seq_len, 128), f32)
    flops = pairs * seq_len * (2 * D * 512 + 12 * 128 * seq_len)
    return pl.pallas_call(
        functools.partial(
            attention_kernel, seq_len=seq_len, rows=rows, groups=groups, fsdp=fsdp, lanes=lanes
        ),
        grid=(pairs,),
        in_specs=[
            pl.BlockSpec(memory_space=pltpu.SMEM),
            whole((seq_len, D), lambda p: (0, 0)),
            whole((seq_len, D), lambda p: (0, 0)),
            pl.BlockSpec((1, 384), lambda p: (0, p)),
            whole((seq_len, 128), lambda p: (0, 0)),
            whole((seq_len, 128), lambda p: (0, 0)),
        ]
        + [pl.BlockSpec(memory_space=pl.ANY)] * fsdp,
        out_specs=[
            pl.BlockSpec((seq_len, 128), lambda p: (0, p)),
            pl.BlockSpec((seq_len, 384), lambda p: (0, p)),
        ],
        out_shape=[
            jax.ShapeDtypeStruct((seq_len, pairs * 128), bf16),
            jax.ShapeDtypeStruct((seq_len, pairs * 384), bf16),
        ],
        scratch_shapes=[
            pltpu.VMEM((D, width), bf16),
            pltpu.VMEM((D + 128, D), bf16),
            pltpu.SemaphoreType.DMA((fsdp, 2)),
        ]
        + [small] * 5 + [turned] * 4 + [wide] * 3,
        compiler_params=pltpu.CompilerParams(vmem_limit_bytes=58 * 1024 * 1024),
        cost_estimate=pl.CostEstimate(
            flops=flops, bytes_accessed=12_000_000, transcendentals=pairs * seq_len * seq_len
        ),
        name="attention",
    )(scalars, attn_in, cot, bias, cos, sin, *pieces)


def mlp_kernel(
    shard_ref,
    rows_ref,
    cot_ref,
    affine_ref,
    bias_ref,
    *refs,
    layout,
    fsdp,
    own_rows,
    unit,
    chunk,
):
    pieces = refs[: len(layout)]
    refs = refs[len(layout) :]
    attn_in_ref, out_ref, grad_in_ref = refs[:3]
    packed_refs = refs[3 : 3 + fsdp]
    mlp_in, mlp_in_t, w_up, w_down, grads_ref, vec_ref, sems, out_sems = refs[3 + fsdp :]
    seq_len = rows_ref.shape[0]
    up_width = fsdp * unit
    folds = unit // own_rows
    rows = 256

    copies = []
    for n, (k, first, count) in enumerate(layout):
        j = shard_ref[0] ^ k
        count = min(count, own_rows - first)
        source = pl.ds(0, count)
        at = pl.ds(pl.multiple_of(j * own_rows + first, 16), count)
        copies.append(
            pltpu.make_async_copy(
                pieces[n].at[source, pl.ds(0, up_width)], w_up.at[at, :], sems.at[n, 0]
            )
        )
        for i in range(folds):
            at = pl.ds(pl.multiple_of(j * unit + i * own_rows + first, 16), count)
            copies.append(
                pltpu.make_async_copy(
                    pieces[n].at[source, pl.ds(up_width + i * D, D)],
                    w_down.at[at, :],
                    sems.at[n, 1 + i],
                )
            )
    for copy in copies:
        copy.start()

    def normed_rows(span):
        x = rows_ref[span, :].astype(f32)
        center = x - jnp.mean(x, -1, keepdims=True)
        return center * lax.rsqrt(jnp.mean(center * center, -1, keepdims=True) + norm_eps)

    def prepare(j, cot_sum):
        span = pl.ds(pl.multiple_of(j * rows, rows), rows)
        normed = normed_rows(span)
        attn_in_ref[span, :] = (normed * affine_ref[0:1, :] + affine_ref[1:2, :]).astype(bf16)
        scaled = normed * affine_ref[2:3, :] + affine_ref[3:4, :]
        mlp_in[span, :] = scaled.astype(bf16)
        mlp_in_t[:, span] = scaled.T.astype(bf16)
        return cot_sum + jnp.sum(cot_ref[span, :].astype(f32), 0, keepdims=True)

    cot_sum = lax.fori_loop(0, seq_len // rows, prepare, jnp.zeros((1, D), f32))
    for copy in copies:
        copy.wait()

    for c in range(up_width // chunk):
        part = slice(c * chunk, (c + 1) * chunk)
        pre_act = dot(mlp_in[...], w_up[:, part]) + bias_ref[:, part]
        cdf = 0.5 + 0.5 * lax.erf(pre_act * inv_sqrt_two)
        hidden = (pre_act * cdf).astype(bf16)
        slope = cdf + pre_act * jnp.exp(-0.5 * pre_act * pre_act) * inv_sqrt_tau
        grad_pre = (dot(cot_ref[...], w_down[part, :], NT) * slope).astype(bf16)
        vec_ref[0:1, part] = jnp.sum(grad_pre.astype(f32), 0, keepdims=True)
        forward = dot(hidden, w_down[part, :])
        backward = dot(grad_pre, w_up[:, part], NT)
        if c == 0:
            out_ref[...] = forward
            grad_in_ref[...] = backward
        else:
            out_ref[...] += forward
            grad_in_ref[...] += backward
        up_grad = dot(mlp_in_t[...], grad_pre).astype(bf16)
        for j in range(fsdp):
            grads_ref[j, :own_rows, part] = up_grad[j * own_rows : (j + 1) * own_rows]
        down_grad = dot(hidden, cot_ref[...], TN).astype(bf16)
        step = math.gcd(own_rows, chunk)
        for r in range(0, chunk, step):
            u = c * chunk + r
            j, i, at = u // unit, u % unit // own_rows, u % own_rows
            grads_ref[j, at : at + step, up_width + i * D : up_width + (i + 1) * D] = down_grad[
                r : r + step
            ]

    def sums(j, carry):
        span = pl.ds(pl.multiple_of(j * rows, rows), rows)
        grad = grad_in_ref[span, :]
        return (
            carry[0] + jnp.sum(grad * normed_rows(span), 0, keepdims=True),
            carry[1] + jnp.sum(grad, 0, keepdims=True),
        )

    none = jnp.zeros((1, D), f32)
    gain_sum, shift_sum = lax.fori_loop(0, seq_len // rows, sums, (none, none))
    row = lax.broadcasted_iota(jnp.int32, (16, D), 0)
    vectors = jnp.where(row == 1, gain_sum, 0.0)
    vectors = jnp.where(row == 2, shift_sum, vectors)
    vectors = jnp.where(row == 3, cot_sum, vectors).astype(bf16)
    row = lax.broadcasted_iota(jnp.int32, (16, unit), 0)
    for j in range(fsdp):
        grads_ref[j, own_rows:, :] = jnp.zeros((16, grads_ref.shape[2]), bf16)
        grads_ref[j, own_rows:, :D] = vectors
        bias = jnp.where(row == 0, vec_ref[0:1, j * unit : (j + 1) * unit], 0.0)
        grads_ref[j, own_rows:, D : D + unit] = bias.astype(bf16)
    copies = [
        pltpu.make_async_copy(
            grads_ref.at[pl.ds(shard_ref[0] ^ k, 1)], packed_refs[k], out_sems.at[k]
        )
        for k in range(fsdp)
    ]
    for copy in copies:
        copy.start()
    for copy in copies:
        copy.wait()


def mlp(shard, rows_in, cot, affine, bias, got, fsdp, unit):
    seq_len = rows_in.shape[0]
    layout = [(k, first, piece.shape[0]) for k, first, piece in got]
    pieces = [piece for _, _, piece in got]
    own_rows = D // fsdp
    packed_width = pieces[0].shape[1]
    up_width = fsdp * unit
    chunk = 256
    vmem = pl.BlockSpec(memory_space=pltpu.VMEM)
    return pl.pallas_call(
        functools.partial(
            mlp_kernel, layout=layout, fsdp=fsdp, own_rows=own_rows, unit=unit, chunk=chunk
        ),
        in_specs=[pl.BlockSpec(memory_space=pltpu.SMEM)]
        + [vmem] * 4
        + [pl.BlockSpec(memory_space=pl.ANY)] * len(pieces),
        out_specs=[vmem] * 3 + [pl.BlockSpec(memory_space=pl.ANY)] * fsdp,
        out_shape=[
            jax.ShapeDtypeStruct((seq_len, D), bf16),
            jax.ShapeDtypeStruct((seq_len, D), f32),
            jax.ShapeDtypeStruct((seq_len, D), f32),
        ]
        + [jax.ShapeDtypeStruct((1, own_rows + 16, packed_width), bf16)] * fsdp,
        scratch_shapes=[
            pltpu.VMEM((seq_len, D), bf16),
            pltpu.VMEM((D, seq_len), bf16),
            pltpu.VMEM((D, up_width), bf16),
            pltpu.VMEM((up_width, D), bf16),
            pltpu.VMEM((fsdp, own_rows + 16, packed_width), bf16),
            pltpu.VMEM((8, up_width), f32),
            pltpu.SemaphoreType.DMA((len(pieces), 1 + unit // own_rows)),
            pltpu.SemaphoreType.DMA((fsdp,)),
        ],
        compiler_params=pltpu.CompilerParams(vmem_limit_bytes=58 * 1024 * 1024),
        cost_estimate=pl.CostEstimate(
            flops=12 * seq_len * D * up_width,
            bytes_accessed=30_000_000,
            transcendentals=2 * seq_len * up_width,
        ),
        name="mlp",
    )(shard, rows_in, cot, affine, bias, *pieces)


def take(x, at, size, axis=0):
    return lax.dynamic_slice_in_dim(x, at * size, size, axis)


def place(out, piece, at, axis=0):
    return lax.dynamic_update_slice_in_dim(out, piece, at * piece.shape[axis], axis)


def swap(x, axis, by):
    n = lax.axis_size(axis)
    return lax.ppermute(x, axis, [(j, j ^ by) for j in range(n)])


def exchange(x, group):
    axis, n, step, me = group
    return [(me ^ s, swap(take(x, me ^ s, 1), axis, s * step) if s else take(x, me, 1)) for s in range(n)]


def gather(x, group):
    axis, n, step, me = group
    return [(me ^ s, swap(x, axis, s * step) if s else x) for s in range(n)]


def gather_rows(x, group):
    axis, n, step, _ = group
    return [(k, 0, swap(x, axis, k * step) if k else x) for k in range(n)]


def stacked(pieces):
    if len(pieces) == 2:
        (me, own), (_, other) = pieces
        first = me == 0
        return jnp.stack([jnp.where(first, own, other), jnp.where(first, other, own)])
    out = jnp.zeros((len(pieces),) + pieces[0][1].shape, pieces[0][1].dtype)
    for j, piece in pieces:
        out = place(out, piece[None], j)
    return out


def after(x, pieces):
    held, arrived = lax.optimization_barrier((x, [piece[-1] for piece in pieces]))
    return held, [piece[:-1] + (got,) for piece, got in zip(pieces, arrived)]


def total(pieces):
    return sum(piece[0].astype(f32) for _, piece in pieces)


def scatter_sum(x, group):
    return total(exchange(x, group))


def rope_tables(seq_len):
    half = ROTARY // 2
    frequency = rope_base ** (-2.0 * np.arange(half) / ROTARY)
    angles = np.arange(seq_len)[:, None] * frequency[None, :]
    cosine, sine = np.cos(angles), np.sin(angles)
    rest = np.zeros((seq_len, HEAD_DIM - ROTARY))
    cos = np.concatenate([cosine, cosine, rest + 1.0] * 2, 1)
    sin = np.concatenate([-sine, sine, rest] * 2, 1)
    return jnp.asarray(cos, f32), jnp.asarray(sin, f32)


def local(
    tokens,
    lengths,
    cotangent,
    qkv_weight,
    qkv_bias,
    out_weight,
    out_bias,
    up_weight,
    up_bias,
    down_weight,
    down_bias,
    attn_gain,
    attn_shift,
    mlp_gain,
    mlp_shift,
):
    seqs, width = tokens.shape[0], tokens.shape[1]
    ctx_size, fsdp = lax.axis_size("ctx"), lax.axis_size("fsdp")
    team = ctx_size // seqs
    here = lax.axis_index("ctx")
    seat, seq = here % team, here // team
    shard = lax.axis_index("fsdp")
    seq_len = ctx_size * width
    heads = HEADS // team
    pairs = (heads + 1) // 2
    lanes = heads * HEAD_DIM
    spare = pairs * 128 - lanes

    def by_pair(x):
        rows = x.shape[0]
        x = take(x.reshape(rows, 3, D), seat, lanes, 2)
        x = jnp.pad(x, ((0, 0), (0, 0), (0, spare)))
        return jnp.concatenate(
            [x[:, t, p * 128 : (p + 1) * 128] for p in range(pairs) for t in range(3)], 1
        )

    unit = FF // (fsdp * team)

    def up_columns(x):
        return jnp.concatenate(
            [take(x[:, j * unit * team : (j + 1) * unit * team], seat, unit, 1) for j in range(fsdp)],
            1,
        )

    seqs_group = ("ctx", seqs, team, seq)
    team_group = ("ctx", team, 1, seat)
    fsdp_group = ("fsdp", fsdp, 1, shard)
    own_rows = D // fsdp
    folds = unit // own_rows

    blocks = [
        jnp.concatenate([take(tokens, seq ^ s, 1), take(cotangent, seq ^ s, 1)]) for s in range(seqs)
    ]
    both = [(seq ^ s, swap(x, "ctx", s * team) if s else x) for s, x in enumerate(blocks)]
    half = stacked(both)
    joined = gather(half, team_group)
    tok_half = half[:, 0]
    rows_in = stacked([(j, h[:, 0]) for j, h in joined]).swapaxes(0, 1).reshape(seq_len, D)
    cot = stacked([(j, h[:, 1]) for j, h in joined]).swapaxes(0, 1).reshape(seq_len, D)

    down_own = take(down_weight, seat, unit)
    mlp_pack = jnp.concatenate(
        [up_columns(up_weight)] + [down_own[i * own_rows : (i + 1) * own_rows] for i in range(folds)],
        1,
    )
    up_width = fsdp * unit
    mlp_width = up_width + folds * D
    vectors = (qkv_bias, out_bias, up_bias, down_bias, attn_gain, attn_shift, mlp_gain, mlp_shift)
    vector_size = sum(v.shape[0] for v in vectors)
    vector_pack = jnp.pad(jnp.concatenate(vectors), (0, mlp_width - vector_size))
    vector_pack = jnp.pad(vector_pack[None], ((0, 31), (0, 0)))
    mlp_pack = jnp.concatenate([mlp_pack, vector_pack], 0)
    mlp_got = gather_rows(mlp_pack, fsdp_group)
    attn_pack = jnp.concatenate([by_pair(qkv_weight), out_weight], 1)
    attn_pack, mlp_got = after(attn_pack, mlp_got)
    attn_got = gather_rows(attn_pack, fsdp_group)
    qkv_width = pairs * 384
    packed = stacked(
        [
            (shard ^ k, piece[own_rows - first, :vector_size])
            for k, first, piece in mlp_got
            if first <= own_rows < first + piece.shape[0]
        ]
    )
    bounds = []
    at = 0
    for v in vectors:
        bounds.append(packed[:, at : at + v.shape[0]].reshape(-1).astype(f32))
        at += v.shape[0]
    full_qkv_b, full_out_b, full_up_b, full_down_b, gain_a, shift_a, gain_m, shift_m = bounds
    b_qkv = by_pair(full_qkv_b[None])
    b_up = up_columns(full_up_b[None])

    def normalise(x):
        x = x.astype(f32)
        center = x - jnp.mean(x, -1, keepdims=True)
        inv = lax.rsqrt(jnp.mean(center * center, -1, keepdims=True) + norm_eps)
        return center * inv, inv

    def columns(x):
        return jnp.sum(x, 0)

    def vector_rows(rows, size):
        out = []
        for at, v in rows:
            v = jnp.broadcast_to(v, (fsdp, v.shape[-1])).astype(bf16)
            out.append(jnp.pad(v, ((0, 0), (at, size - at - v.shape[1])))[:, None])
        return jnp.pad(jnp.concatenate(out, 1), ((0, 0), (0, 16 - len(rows)), (0, 0)))

    normed, _ = normalise(rows_in)
    if seq_len <= 2048:
        affine = jnp.concatenate(
            [gain_a[None], shift_a[None], gain_m[None], shift_m[None], jnp.zeros((4, D), f32)]
        )
        attn_in, mlp_out, grad_mlp_in, *mlp_grads = mlp(
            shard.reshape(1).astype(jnp.int32),
            rows_in,
            cot,
            affine,
            b_up,
            mlp_got,
            fsdp,
            unit,
        )
    else:
        w_up = jnp.zeros((D, up_width), bf16)
        w_down = jnp.zeros((fsdp, folds, own_rows, D), bf16)
        for k, _, piece in mlp_got:
            w_up = place(w_up, piece[:own_rows, :up_width], shard ^ k)
            for i in range(folds):
                part = piece[:own_rows, up_width + i * D : up_width + (i + 1) * D]
                w_down = lax.dynamic_update_slice(w_down, part[None, None], (shard ^ k, i, 0, 0))
        w_down = w_down.reshape(up_width, D)
        attn_in = (normed * gain_a + shift_a).astype(bf16)
        mlp_in = (normed * gain_m + shift_m).astype(bf16)

        pre_act = dot(mlp_in, w_up) + b_up
        cdf = 0.5 * (1.0 + lax.erf(pre_act * inv_sqrt_two))
        hidden = (pre_act * cdf).astype(bf16)
        slope = cdf + pre_act * jnp.exp(-0.5 * pre_act * pre_act) * inv_sqrt_tau
        grad_pre = (dot(cot, w_down, NT) * slope).astype(bf16)
        down_grad = dot(hidden, cot, TN)
        up_grad = dot(mlp_in, grad_pre, TN)
        mlp_out = dot(hidden, w_down)
        grad_mlp_in = dot(grad_pre, w_up, NT)

        mlp_grads = jnp.concatenate(
            [up_grad.astype(bf16).reshape(fsdp, own_rows, up_width)]
            + [
                down_grad.astype(bf16).reshape(fsdp, folds, own_rows, D)[:, i] for i in range(folds)
            ],
            2,
        )
        rows = vector_rows(
            [
                (D, columns(grad_pre.astype(f32)).reshape(fsdp, unit)),
                (0, columns(grad_mlp_in * normed)),
                (0, columns(grad_mlp_in)),
                (0, columns(cot.astype(f32))),
            ],
            mlp_width,
        )
        mlp_grads = jnp.concatenate([mlp_grads, rows], 1)
        mlp_grads = [take(mlp_grads, shard ^ k, 1) for k in range(fsdp)]

    def halve(mine):
        cols = mine.shape[1] // seqs
        block = [take(mine, seq ^ k, cols, 1) for k in range(seqs)]
        got = swap(jnp.stack([block[1], block[3]]), "ctx", team)
        return block[0], block[2], got

    def quarter(own, far, got):
        own = own.astype(f32) + got[0].astype(f32)
        far = far.astype(f32) + got[1].astype(f32)
        return (own + swap(far.astype(bf16), "ctx", 2 * team).astype(f32)).astype(bf16)

    def widen(part):
        return jnp.stack([part, swap(part, "ctx", 2 * team)])

    def whole_again(two):
        got = swap(two, "ctx", team)
        rows, cols = two.shape[1:]
        whole = jnp.zeros((rows, seqs * cols), bf16)
        for k, piece in ((0, two[0]), (2, two[1]), (1, got[0]), (3, got[1])):
            whole = place(whole, piece, seq ^ k, 1)
        return stacked(gather(whole, team_group))

    attn_in, cot_held, mlp_grads, attn_got = lax.optimization_barrier(
        (attn_in, cot, list(mlp_grads), [piece for _, _, piece in attn_got])
    )
    mlp_pieces = [
        (shard ^ k, swap(x, "fsdp", k) if k else x) for k, x in enumerate(mlp_grads)
    ]
    scalars = jnp.stack([lax.dynamic_index_in_dim(lengths, seq, 0, False), shard, seat])
    mixed, grad_proj = attention(
        scalars.astype(jnp.int32), attn_in, cot_held, attn_got, b_qkv, *rope_tables(seq_len), lanes
    )
    (mixed, grad_proj, attn_got), mlp_pieces = after((mixed, grad_proj, attn_got), mlp_pieces)
    mlp_mine = total(mlp_pieces).astype(bf16)
    mixed, grad_proj, mlp_mine = lax.optimization_barrier((mixed, grad_proj, mlp_mine))
    mlp_own, mlp_far, mlp_near = halve(mlp_mine)

    w_qkv = jnp.zeros((D, qkv_width), bf16)
    w_out = jnp.zeros((D, D), bf16)
    for k, piece in enumerate(attn_got):
        w_qkv = place(w_qkv, piece[:, :qkv_width], shard ^ k)
        w_out = place(w_out, piece[:, qkv_width:], shard ^ k)
    w_out_rows = jnp.pad(take(w_out, seat, lanes), ((0, spare), (0, 0)))
    delta_out = mlp_out + dot(mixed, w_out_rows)
    mixed_got = gather(mixed[:, :lanes], team_group)
    grad_proj, mlp_near = lax.optimization_barrier((grad_proj, mlp_near))
    mlp_part = quarter(mlp_own, mlp_far, mlp_near)
    grad_attn_in = dot(grad_proj, w_qkv, NT)
    qkv_grad = dot(attn_in, grad_proj, TN)
    out_cols = D // team
    cot_cols = take(cot, seat, out_cols, 1)
    out_grad = stacked([(j, dot(m, cot_cols, TN).astype(bf16)) for j, m in mixed_got])

    qkv_b_grad = columns(grad_proj.astype(f32))
    qkv_b_grad = jnp.concatenate(
        [
            jnp.concatenate(
                [
                    qkv_b_grad[p * 384 + i * 128 : p * 384 + i * 128 + min(128, lanes - p * 128)]
                    for p in range(pairs)
                ]
            )[None]
            for i in range(3)
        ],
        0,
    )
    qkv_b_grad = place(jnp.zeros((3, D), f32), qkv_b_grad, seat, 1)
    attn_width = qkv_width + out_cols
    attn_grads = jnp.concatenate(
        [
            qkv_grad.astype(bf16).reshape(fsdp, own_rows, qkv_width),
            out_grad.astype(bf16).reshape(fsdp, own_rows, out_cols),
        ],
        2,
    )
    attn_grads = jnp.concatenate(
        [
            attn_grads,
            vector_rows(
                [
                    (0, qkv_b_grad.reshape(fsdp, -1)),
                    (0, columns(grad_attn_in * normed)),
                    (0, columns(grad_attn_in)),
                ],
                attn_width,
            ),
        ],
        1,
    )

    def home(x):
        return scatter_sum(x.astype(bf16).reshape(seqs, team, width, D).swapaxes(0, 1), team_group)

    def returned(pieces):
        return stacked([(j, piece[0]) for j, piece in pieces])

    delta_out, mlp_part = lax.optimization_barrier((home(delta_out).astype(bf16), mlp_part))
    out_pieces = exchange(delta_out, seqs_group)

    grad_normed = home(grad_attn_in * gain_a + grad_mlp_in * gain_m)
    attn_grads, grad_normed = lax.optimization_barrier((attn_grads, grad_normed))
    attn_pieces = exchange(attn_grads, fsdp_group)
    normed_half, inv_half = normalise(tok_half)
    delta_in = inv_half * (
        grad_normed
        - jnp.mean(grad_normed, -1, keepdims=True)
        - normed_half * jnp.mean(grad_normed * normed_half, -1, keepdims=True)
    )
    mlp_part, attn_pieces = after(mlp_part, attn_pieces)
    mlp_two = widen(mlp_part)
    attn_own, attn_far, attn_near = halve(total(attn_pieces).astype(bf16))
    delta_in, attn_near = lax.optimization_barrier((delta_in.astype(bf16), attn_near))
    delta_in, out_pieces = after(delta_in, out_pieces)
    in_pieces = exchange(delta_in, seqs_group)
    layer_out = (
        tokens.astype(f32) + returned(out_pieces).astype(f32) + full_out_b + full_down_b
    ).astype(bf16)

    mlp_all = whole_again(mlp_two)
    tokens_grad = cotangent.astype(f32) + returned(in_pieces).astype(f32)
    attn_all = whole_again(widen(quarter(attn_own, attn_far, attn_near)))

    up_mine = jnp.concatenate(
        [
            mlp_all[t, :own_rows, j * unit : (j + 1) * unit]
            for j in range(fsdp)
            for t in range(team)
        ],
        1,
    ).astype(f32)
    down_mine = jnp.concatenate(
        [
            mlp_all[t, :own_rows, up_width + i * D : up_width + (i + 1) * D]
            for t in range(team)
            for i in range(folds)
        ],
        0,
    ).astype(f32)
    qkv_mine = jnp.concatenate(
        [
            attn_all[
                t, :own_rows, p * 384 + i * 128 : p * 384 + i * 128 + min(128, lanes - p * 128)
            ]
            for i in range(3)
            for t in range(team)
            for p in range(pairs)
        ],
        1,
    ).astype(f32)
    out_mine = jnp.concatenate([attn_all[t, :own_rows, qkv_width:] for t in range(team)], 1).astype(f32)
    mlp_vec = mlp_all[:, own_rows : own_rows + 4].astype(f32)
    up_b_mine = mlp_vec[:, 0, D : D + unit].reshape(-1)
    mlp_vec = take(jnp.sum(mlp_vec[:, 1:, :D], 0), shard, own_rows, 1)
    bias_mine = mlp_vec[2] * (1.0 / team)
    attn_vec = jnp.sum(attn_all[:, own_rows : own_rows + 3].astype(f32), 0)
    qkv_b_mine = attn_vec[0, : 3 * own_rows]
    attn_vec = take(attn_vec[1:, :D], shard, own_rows, 1)

    return (
        layer_out,
        tokens_grad,
        qkv_mine,
        qkv_b_mine,
        out_mine,
        bias_mine,
        up_mine,
        up_b_mine,
        down_mine,
        bias_mine,
        attn_vec[0],
        attn_vec[1],
        mlp_vec[0],
        mlp_vec[1],
    )


def solution(mesh):
    rows, whole = P("fsdp", "ctx", None), P("fsdp", None)
    vector = P("fsdp")
    in_specs = (
        rows,
        vector,
        rows,
        whole,
        vector,
        whole,
        vector,
        whole,
        vector,
        whole,
        vector,
        vector,
        vector,
        vector,
        vector,
    )
    out_specs = (
        rows,
        rows,
        whole,
        vector,
        whole,
        vector,
        whole,
        vector,
        whole,
        vector,
        vector,
        vector,
        vector,
        vector,
    )
    return jax.shard_map(local, mesh=mesh, in_specs=in_specs, out_specs=out_specs, check_vma=False)
```
